32 devices in a mesh: mpo: 2 (over x), sector: 16 (over z, y, core).
Axes of the slice: x: 2, y: 2, z: 4, core: 2. Of those that a mesh axis runs over, the one named last changes fastest.
Arguments:
- wavefunction: bfloat16 [64, 512, 512], P('sector'), may hold values from -6 to 6
- left_env: bfloat16 [2, 64, 512, 512], P('mpo', 'sector'), may hold values from -0.375 to 0.375
- right_env: bfloat16 [2, 64, 512, 512], P('mpo', 'sector'), may hold values from -0.1875 to 0.1875
- mpo_mask: int32 [2, 64], P('mpo', 'sector'), may hold values 0 or 1
- block_size: int32 [64], P('sector'), may hold values from 64 to 512, as said below
- route_owner: int32 [2, 64, 8], P('mpo', 'sector'), may hold values from 0 to 15, all different within a row; in each aligned block of 4 rows (0 to 3, 4 to 7, ..., all dimensions but the last counted through in order) at most 4 rows name the same one
- route_block: int32 [2, 64, 8], P('mpo', 'sector'), may hold values from 0 to 3
Outputs:
- sigma_right: bfloat16 [64, 512, 512], P('sector', 'mpo')
The draws below stay inside these ranges and needn't reach their ends.
Inputs may be any that keep to these rules, and one draw needn't show every extreme that they name: `block_size`: some block in every draw has all 512 states live. `route_owner`: each row (m, b) names 8 different owners. Among the 4 rows of one device (one m and the blocks of one sector owner) no owner is named more than 4 times, and in some device's rows some owner is named exactly 4 times; every owner is named somewhere.
All inputs are finite; a program needn't handle non-finite values. No bound on the sum of `mpo_mask` on one device may be relied on, other than what follows from the above.
Results may differ from the reference program's by a relative error of at most 0.014.
Values may be sent and summed in bfloat16 or wider, within the bound.
No kernel may reach another device: no remote copies, remote signals or barrier semaphores. Data moves between devices by JAX's collectives and lax.ppermute only.
A program may use at most 64 MiB of HBM per device.

```python
import math
import jax
import jax.numpy as jnp
import numpy as np
from jax import lax

STATES = 512
NB_DEV = 4
ROW_GROUPS = 4
COL_PARTS = 2
PIECES = 8
CAP = 4
NBLOCKS = 64
BONDS = 2
N_MPO = 2
N_SECTOR = 16


def draw_block_size(key, part):
    key_sizes, key_pick = jax.random.split(jax.random.fold_in(key, 17))
    drawn = jax.random.randint(key_sizes, (NBLOCKS,), STATES // 8, STATES + 1, dtype=jnp.int32)
    chosen = jax.random.randint(key_pick, (), 0, NBLOCKS, dtype=jnp.int32)
    return jnp.where(jnp.arange(NBLOCKS, dtype=jnp.int32) == chosen, STATES, drawn).astype(jnp.int32)


def plant(values, own_key, low, largest):
    longest = values.shape.index(max(values.shape))
    spots = []
    for shift in (0, 1):
        where = [jax.random.randint(jax.random.fold_in(own_key, axis), (), 0, length) for axis, length in enumerate(values.shape)]
        where[longest] = (where[longest] + shift) % values.shape[longest]
        spots.append(tuple(where))
    return values.at[spots[0]].set(low).at[spots[1]].set(largest)


def spiked(values, key, source, target, blocks, factor):
    def block_of(position):
        return (jnp.arange(values.shape[position]) // (values.shape[position] // blocks)).reshape((-1,) + (1,) * (values.ndim - 1 - position))

    near = jax.random.permutation(key, blocks)[block_of(target)]
    other_side = (block_of(target) + blocks // 2) % blocks
    return jnp.where((block_of(source) == near) | (block_of(source) == other_side), factor * values, values)


def steps_of(stream_key, dims, cuts, low, largest):
    def one(position, parts):
        heights = jax.random.uniform(jax.random.fold_in(jax.random.fold_in(stream_key, 6), position), (parts,), jnp.float32, low / len(cuts), largest / len(cuts))
        return jnp.repeat(jnp.exp(heights), dims[position] // parts).reshape((-1,) + (1,) * (len(dims) - position - 1))

    factor_of = one(*cuts[0])
    for cut in cuts[1:]:
        factor_of = factor_of * one(*cut)
    return factor_of


def routed_block(key, own, number, rows, number_of, top, limit, skew):
    sequence = jax.random.permutation(key, number_of)
    heavy_load, common = load_shares(number_of, rows * top, limit, skew, True), load_shares(number_of, rows * top, limit, skew, False)
    places = jnp.arange(number_of)

    def named(tallies, rotation):
        used = int((tallies > 0).sum())
        fixed = max(1, used // 4)
        moved = fixed + (places - fixed + rotation * (used - fixed)) % max(1, number_of - fixed)
        return jnp.zeros((number_of,), jnp.int32).at[sequence[jnp.where(places < fixed, places, moved)]].set(jnp.asarray(tallies, jnp.int32))

    tallies = jnp.where(number % 4 == 0, named(heavy_load, number // 4), named(common, number - number // 4 - 1))
    mixed = jax.random.permutation(jax.random.fold_in(own, 3), number_of)
    source_of, taker = mixed[0:number_of // 2 * 2:2], mixed[1:number_of // 2 * 2:2]
    slack = jnp.minimum(tallies[source_of] - 1, limit - tallies[taker]) // 2
    slack = jnp.where((source_of == sequence[0]) | (taker == sequence[0]) | (tallies[taker] == 0), 0, jnp.maximum(slack, 0))
    moved = jax.random.randint(jax.random.fold_in(own, 4), (number_of // 2,), 0, 1 << 20) % (slack + 1)
    tallies = tallies.at[source_of].add(-moved).at[taker].add(moved)
    items = jnp.searchsorted(jnp.cumsum(tallies), jnp.arange(rows * top), side="right").astype(jnp.int32)
    listing = items.reshape(top, rows).T
    listing = listing[jax.random.permutation(jax.random.fold_in(own, 1), rows)]
    rotation = jax.random.randint(jax.random.fold_in(own, 2), (rows, 1), 0, top)
    return jnp.take_along_axis(listing, (jnp.arange(top)[None, :] + rotation) % top, axis=1)


def load_shares(amount, total, most, lean, full):
    weights = [(1 << 20) // math.isqrt(rank ** lean) + 1 for rank in range(1, amount + 1)]
    largest = most if full else min(most, max(-(-total // amount), total * weights[0] // sum(weights)))
    least = 1 if total - largest >= amount - 1 else 0
    holding, spare = [largest] + [least] * (amount - 1), total - largest - least * (amount - 1)
    while spare > 0:
        free = [i for i in range(1, amount) if holding[i] < largest] or [i for i in range(1, amount) if holding[i] < most]
        mass, remaining = sum([weights[i] for i in free]), spare
        for i in free:
            more = min(most - holding[i], max(1, remaining * weights[i] // mass), spare)
            holding[i] = holding[i] + more
            spare = spare - more
    return np.array(holding)


def gaussian(stream_key, extent, scale, bound, cuts=(), held_as=jnp.bfloat16):
    values = scale * jax.random.normal(stream_key, extent, jnp.float32)
    if cuts:
        values = values * steps_of(stream_key, extent, cuts, -0.22, 0.18)
    return jnp.clip(values, -bound, bound).astype(held_as)


def heavy_noise(stream_key, extent, width, most, cuts, heavy, kind=jnp.bfloat16):
    values = width * jax.random.normal(stream_key, extent, jnp.float32)
    if cuts:
        values = values * steps_of(stream_key, extent, cuts, -0.22, 0.18)
    return jnp.clip(spiked(values, jax.random.fold_in(stream_key, 3), *heavy), -most, most).astype(kind)


def setup_inputs(seed: int = 0) -> dict:
    key_list = jax.random.split(jax.random.key(seed), 8)
    wavefunction = gaussian(key_list[0], (NBLOCKS, STATES, STATES), 1.0, 6.0, ((0, 16),))
    left_env = heavy_noise(key_list[1], (BONDS, NBLOCKS, STATES, STATES), STATES ** -0.5, 0.375, ((0, 2), (1, 16)), (0, 2, 2, 2.0))
    right_env = gaussian(key_list[2], (BONDS, NBLOCKS, STATES, STATES), (STATES * BONDS) ** -0.5, 0.1875, ((0, 2), (1, 16)))
    mpo_mask = plant((jax.random.randint(key_list[3], (BONDS, NBLOCKS), 0, 4) < 3).astype(jnp.int32), jax.random.fold_in(key_list[3], 1), 0, 1)
    block_size = draw_block_size(jax.random.fold_in(key_list[7], 71), 0)
    route_owner_keys = jax.random.split(jax.random.fold_in(key_list[5], 1), BONDS * NBLOCKS // NB_DEV)
    route_owner_turns = jax.random.permutation(jax.random.fold_in(key_list[5], 3), BONDS * NBLOCKS // NB_DEV)
    route_owner = jax.vmap(lambda own, number: routed_block(jax.random.fold_in(key_list[5], 2), own, number, NB_DEV, N_SECTOR, PIECES, CAP, 2))(route_owner_keys, route_owner_turns).reshape((BONDS, NBLOCKS, PIECES))
    route_block = plant(jax.random.randint(key_list[6], (BONDS, NBLOCKS, PIECES), 0, NB_DEV), jax.random.fold_in(key_list[6], 1), 0, NB_DEV - 1).astype(jnp.int32)
    return dict(wavefunction=wavefunction, left_env=left_env, right_env=right_env, mpo_mask=mpo_mask, block_size=block_size, route_owner=route_owner, route_block=route_block)


def reference(wavefunction, left_env, right_env, mpo_mask, block_size, route_owner, route_block):
    nblocks = wavefunction.shape[0]
    states = wavefunction.shape[1]
    positions = jnp.arange(states, dtype=jnp.int32)
    live_rows = positions[None, :] < block_size[:, None]
    live_mask = live_rows[:, :, None] & live_rows[:, None, :]
    masked = jnp.where(live_mask, wavefunction, jnp.zeros_like(wavefunction))

    def one_index(running, inputs):
        left_slice, right_slice, mask_slice = inputs
        right_part = jnp.einsum("bij,bkj->bik", masked.astype(jnp.float32), right_slice.astype(jnp.float32)).astype(jnp.bfloat16)
        product = jnp.einsum("bij,bjk->bik", left_slice.astype(jnp.float32), right_part.astype(jnp.float32))
        product = product * mask_slice.astype(jnp.float32)[:, None, None]
        rounded = lax.optimization_barrier(product.astype(jnp.bfloat16))
        return running + rounded.astype(jnp.float32), None

    summed, _ = lax.scan(one_index, jnp.zeros(wavefunction.shape, jnp.float32), (left_env, right_env, mpo_mask))
    sigma_left = jnp.where(live_mask, summed, jnp.zeros_like(summed)).astype(jnp.bfloat16)

    group_rows = states // (N_MPO * ROW_GROUPS)
    width_part = states // COL_PARTS
    pieces = sigma_left.reshape(nblocks, N_MPO, ROW_GROUPS, group_rows, COL_PARTS, width_part)
    pieces = pieces.transpose(1, 0, 2, 4, 3, 5).reshape(N_MPO, nblocks, PIECES, group_rows, width_part)
    target = (route_owner * NB_DEV + route_block).astype(jnp.int32)
    piece_ids = jnp.arange(PIECES, dtype=jnp.int32)[None, None, :]
    mpo_ids = jnp.arange(N_MPO, dtype=jnp.int32)[:, None, None]
    result = jnp.zeros((nblocks, N_MPO, PIECES, group_rows, width_part), jnp.float32)
    result = result.at[target, mpo_ids, piece_ids].add(pieces.astype(jnp.float32))
    result = result.reshape(nblocks, N_MPO, ROW_GROUPS, COL_PARTS, group_rows, width_part)
    result = result.transpose(0, 1, 2, 4, 3, 5).reshape(nblocks, states, states)
    return result.astype(jnp.bfloat16)
```

```python
import functools

import jax
import jax.numpy as jnp
from jax import lax
from jax.experimental import pallas as pl
from jax.experimental.pallas import tpu as pltpu
from jax.sharding import PartitionSpec as P

ROW_GROUPS = 4
COL_PARTS = 2
PIECES = 8
SLOTS = 2
SPILL = 3
PHASES = 2
LANES = 128
INFO = 16

VMEM = pl.BlockSpec(memory_space=pltpu.VMEM)
SMEM = pl.BlockSpec(memory_space=pltpu.SMEM)
ANY = pl.BlockSpec(memory_space=pl.ANY)


def params(mib):
    return pltpu.CompilerParams(vmem_limit_bytes=mib * 2**20)


def exchange_all(sigma_share, route_owner, route_block):
    row_count, block_count, states = sigma_share.shape
    group_rows = row_count // ROW_GROUPS
    width_part = states // COL_PARTS
    pieces = sigma_share.reshape(ROW_GROUPS, group_rows, block_count, COL_PARTS, width_part)
    pieces = pieces.transpose(2, 0, 3, 1, 4).reshape(block_count * PIECES, group_rows * width_part)
    owners = route_owner[0].reshape(-1)
    target_code = (route_block[0] * PIECES + jnp.arange(PIECES, dtype=jnp.int32)[None, :]).reshape(-1)
    peer_count = lax.axis_size("sector")
    capacity = min(block_count, max(2, (2 * block_count * PIECES + peer_count - 1) // peer_count))
    is_owner = (owners[:, None] == jnp.arange(peer_count, dtype=jnp.int32)[None, :]).astype(jnp.int32)
    before = jnp.cumsum(is_owner, axis=0) - is_owner
    position = jnp.sum(before * is_owner, axis=1)
    destination = owners * capacity + position
    slot_ids = jnp.arange(peer_count * capacity, dtype=jnp.int32)
    placing = slot_ids[:, None] == destination[None, :]
    send_data = jnp.dot(placing.astype(jnp.bfloat16), pieces, preferred_element_type=jnp.float32).astype(jnp.bfloat16)
    send_data = send_data.reshape(peer_count, capacity, group_rows * width_part)
    send_code = (jnp.sum(placing.astype(jnp.int32) * (target_code + 1)[None, :], axis=1) - 1).reshape(peer_count, capacity)
    arrived_data, arrived_code = (
        lax.all_to_all(send_data, "sector", split_axis=0, concat_axis=0, tiled=True),
        lax.all_to_all(send_code, "sector", split_axis=0, concat_axis=0, tiled=True),
    )
    arrived_data = arrived_data.reshape(peer_count * capacity, group_rows * width_part)
    arrived_code = arrived_code.reshape(-1)
    targets = jnp.arange(block_count * PIECES, dtype=jnp.int32)
    collect = (arrived_code[None, :] == targets[:, None]).astype(jnp.bfloat16)
    landed = jnp.dot(collect, arrived_data, preferred_element_type=jnp.float32).astype(jnp.bfloat16)
    landed = landed.reshape(block_count, ROW_GROUPS, COL_PARTS, group_rows, width_part)
    return landed.transpose(0, 1, 3, 2, 4).reshape(block_count, row_count, states)


def general(wavefunction, left_env, right_env, mpo_mask, block_size, route_owner, route_block):
    states = wavefunction.shape[1]
    row_count = states // lax.axis_size("mpo")
    positions = jnp.arange(states, dtype=jnp.int32)
    live_cols = positions[None, :] < block_size[:, None]
    live_mask = live_cols[:, :, None] & live_cols[:, None, :]
    masked = jnp.where(live_mask, wavefunction, jnp.zeros_like(wavefunction))
    right_part = jnp.einsum("bij,bkj->bik", masked, right_env[0], preferred_element_type=jnp.float32).astype(jnp.bfloat16)
    factor = mpo_mask[0].astype(jnp.float32)
    product = jnp.einsum("bij,bjk->ibk", left_env[0], right_part, preferred_element_type=jnp.float32)
    row_share = lax.psum_scatter(
        (product * factor[None, :, None]).astype(jnp.bfloat16), "mpo", scatter_dimension=0, tiled=True
    ).astype(jnp.float32)
    global_rows = lax.axis_index("mpo") * row_count + jnp.arange(row_count, dtype=jnp.int32)
    live_rows = global_rows[:, None] < block_size[None, :]
    share_mask = live_rows[:, :, None] & live_cols[None, :, :]
    sigma_share = jnp.where(share_mask, row_share, jnp.zeros_like(row_share)).astype(jnp.bfloat16)
    return exchange_all(sigma_share, route_owner, route_block)


def route_kernel(peers, blocks, group_rows, width, place_ref, owner_ref, block_ref, size_ref, src_ref, info_ref, count):
    first_row = place_ref[0] * (ROW_GROUPS * group_rows)

    def clear(i, _):
        src_ref[i] = -1
        info_ref[i] = -1
        return 0

    lax.fori_loop(0, LANES, clear, 0)

    def clear_count(i, _):
        count[i] = 0
        return 0

    lax.fori_loop(0, peers, clear_count, 0)
    spill_at = peers * SLOTS

    def one(i, spilled):
        b, k = i // PIECES, i % PIECES
        g, c = k // COL_PARTS, k % COL_PARTS
        size = size_ref[b]
        live = (first_row + g * group_rows < size) & (c * width < size)
        owner = owner_ref[i]
        pos = count[owner]
        index = (b * COL_PARTS + c) * ROW_GROUPS + g
        code = block_ref[i] * PIECES + k
        direct = live & (pos < SLOTS)
        spills = live & (pos >= SLOTS)

        @pl.when(direct)
        def _():
            src_ref[owner * SLOTS + pos] = index
            info_ref[owner * SLOTS + pos] = code
            count[owner] = pos + 1

        @pl.when(spills & (spilled < SPILL))
        def _():
            src_ref[spill_at + spilled] = index
            info_ref[spill_at + spilled] = owner
            info_ref[spill_at + SPILL + spilled] = code

        return spilled + spills.astype(jnp.int32)

    spilled = lax.fori_loop(0, blocks * PIECES, one, 0)
    src_ref[LANES - 1] = (spilled > SPILL).astype(jnp.int32)


def term_kernel(share, width, place_ref, size_ref, mask_ref, wave_ref, left_ref, right_ref, own_ref, send_ref, phase):
    b = pl.program_id(0)
    mine = place_ref[0]
    size = size_ref[b]
    active = mask_ref[b] != 0
    states = wave_ref.shape[1]
    span = right_ref.shape[3]
    rows = lax.broadcasted_iota(jnp.int32, (states, states), 0)
    cols = lax.broadcasted_iota(jnp.int32, (states, states), 1)
    masked = jnp.where((rows < size) & (cols < size), wave_ref[0], jnp.zeros_like(wave_ref[0]))
    right = right_ref[0, :, 0].reshape(COL_PARTS * span, states)
    part = lax.dot_general(masked, right, (((1,), (1,)), ((), ())), preferred_element_type=jnp.float32).astype(jnp.bfloat16)
    row = lax.broadcasted_iota(jnp.int32, (share, COL_PARTS * span), 0)
    lane = lax.broadcasted_iota(jnp.int32, (share, COL_PARTS * span), 1)
    col = (lane // span) * width + phase * span + lane % span
    for target, half in ((send_ref, 1 - mine), (own_ref, mine)):
        start = pl.multiple_of(half * share, share)
        product = jnp.dot(left_ref[0, pl.ds(start, share), :], part, preferred_element_type=jnp.float32)
        keep = (row + start < size) & (col < size) & active
        product = jnp.where(keep, product, 0.0).astype(jnp.bfloat16)
        for c in range(COL_PARTS):
            target[0, c] = product[:, c * span : (c + 1) * span]


def terms(place, sizes, mask, wave, left, right, phase, share):
    blocks, states, _ = wave.shape
    width = states // COL_PARTS
    span = width // PHASES
    right = right.reshape(blocks, COL_PARTS, PHASES, span, states)
    out = jax.ShapeDtypeStruct((blocks, COL_PARTS, share, span), jnp.bfloat16)
    out_spec = pl.BlockSpec((1, COL_PARTS, share, span), lambda b, *_: (b, 0, 0, 0))
    body = functools.partial(term_kernel, share, width, phase=phase)
    return pl.pallas_call(
        body,
        grid_spec=pltpu.PrefetchScalarGridSpec(
            num_scalar_prefetch=3,
            grid=(blocks,),
            in_specs=[
                pl.BlockSpec((1, states, states), lambda b, *_: (b, 0, 0)),
                pl.BlockSpec((1, states, states), lambda b, *_: (b, 0, 0)),
                pl.BlockSpec((1, COL_PARTS, 1, span, states), lambda b, *_: (b, 0, phase, 0, 0)),
            ],
            out_specs=[out_spec, out_spec],
        ),
        out_shape=[out, out],
        compiler_params=params(40),
        cost_estimate=pl.CostEstimate(
            flops=4 * blocks * states * states * width, bytes_accessed=6 * blocks * states * states, transcendentals=0
        ),
        name="terms",
    )(place, sizes, mask, wave, left, right)


def pick_kernel(rows, src_ref, *refs):
    sources, out_ref, sems = refs[:PHASES], refs[PHASES], refs[PHASES + 1]
    copies = []
    for p in range(PHASES):
        for j in range(SPILL):
            at = pl.multiple_of(jnp.maximum(src_ref[j], 0) * rows, rows)
            to = (p * SPILL + j) * rows
            copies.append(pltpu.make_async_copy(sources[p].at[pl.ds(at, rows)], out_ref.at[pl.ds(to, rows)], sems.at[p * SPILL + j]))
    for copy in copies:
        copy.start()
    for copy in copies:
        copy.wait()


def pick(src, arrays, rows):
    return pl.pallas_call(
        functools.partial(pick_kernel, rows),
        in_specs=[SMEM] + [ANY] * PHASES,
        out_specs=VMEM,
        out_shape=jax.ShapeDtypeStruct((PHASES * SPILL * rows, LANES), jnp.bfloat16),
        scratch_shapes=[pltpu.SemaphoreType.DMA((PHASES * SPILL,))],
        compiler_params=params(16),
        name="pick",
    )(src, *arrays)


def spill_kernel(mine_ref, other_ref, info_ref, out_ref):
    count = mine_ref.shape[0]
    out_ref[:count] = (mine_ref[...].astype(jnp.float32) + other_ref[...].astype(jnp.float32)).astype(jnp.bfloat16)
    out_ref[count:] = info_ref[...]


def pack_kernel(rows, slots, src_ref, own_ref, other_ref, out_ref):
    def one(j, _):
        index = src_ref[j]

        @pl.when(index >= 0)
        def _():
            at = pl.ds(pl.multiple_of(index * rows, rows), rows)
            total = own_ref[at, :].astype(jnp.float32) + other_ref[at, :].astype(jnp.float32)
            out_ref[pl.ds(pl.multiple_of(j * rows, rows), rows), :] = total.astype(jnp.bfloat16)

        return 0

    lax.fori_loop(0, slots, one, 0)


def pack(src, own, other, rows, slots):
    return pl.pallas_call(
        functools.partial(pack_kernel, rows, slots),
        in_specs=[SMEM, VMEM, VMEM],
        out_specs=VMEM,
        out_shape=jax.ShapeDtypeStruct((slots * rows, LANES), jnp.bfloat16),
        compiler_params=params(16),
        name="pack",
    )(src, own, other)


def add_spilled(rows, peers, phase, place_ref, info_ref, sets, acc):
    me = place_ref[1]
    spill_at = peers * SLOTS
    chunk = PHASES * SPILL * rows + INFO
    each = peers // len(sets)
    for which, ref in enumerate(sets):

        def one(i, _, which=which, ref=ref):
            source, j = i // SPILL, i % SPILL
            table = which * each + source

            @pl.when(info_ref[table, spill_at + j] == me)
            def _():
                code = info_ref[table, spill_at + SPILL + j]
                start = source * chunk + (phase * SPILL + j) * rows
                at = pl.ds(pl.multiple_of(start, 16), rows)
                to = pl.ds(pl.multiple_of(code * rows, rows), rows)
                acc[to, :] += ref[at, :].astype(jnp.float32)

            return 0

        lax.fori_loop(0, each * SPILL, one, 0)


def add_direct(rows, peers, place_ref, info_ref, arrived_ref, acc):
    me = place_ref[1]
    quarter = peers // 4

    def one(j, _):
        source, slot = j // SLOTS, j % SLOTS
        apart = source ^ me
        table = ((apart & 1) * 2 + ((apart >> 1) & 1)) * quarter + (apart >> 2)
        code = info_ref[table, me * SLOTS + slot]

        @pl.when(code >= 0)
        def _():
            at = pl.ds(pl.multiple_of(j * rows, rows), rows)
            to = pl.ds(pl.multiple_of(code * rows, rows), rows)
            acc[to, :] += arrived_ref[at, :].astype(jnp.float32)

        return 0

    lax.fori_loop(0, peers * SLOTS, one, 0)


def early_kernel(rows, peers, place_ref, info_ref, arrived_ref, *refs):
    sets, done_ref, later_ref, acc = refs[:4], refs[4], refs[5], refs[6]
    acc[...] = jnp.zeros_like(acc)
    later_ref[...] = jnp.zeros_like(later_ref)
    add_spilled(rows, peers, 0, place_ref, info_ref, sets, acc)
    add_spilled(rows, peers, 1, place_ref, info_ref, sets, later_ref)
    add_direct(rows, peers, place_ref, info_ref, arrived_ref, acc)
    done_ref[...] = acc[...].astype(jnp.bfloat16)


def late_kernel(rows, peers, place_ref, info_ref, arrived_ref, done_ref, later_ref, out_ref, acc):
    acc[...] = later_ref[...]
    add_direct(rows, peers, place_ref, info_ref, arrived_ref, acc)
    width = out_ref.shape[2] // COL_PARTS
    span = width // PHASES
    for t in range(out_ref.shape[0]):
        for k in range(PIECES):
            g, c = k // COL_PARTS, k % COL_PARTS
            at = slice((t * PIECES + k) * rows, (t * PIECES + k + 1) * rows)
            out_ref[t, g * rows : (g + 1) * rows, c * width : c * width + span] = done_ref[at, :]
            out_ref[t, g * rows : (g + 1) * rows, c * width + span : (c + 1) * width] = acc[at, :].astype(jnp.bfloat16)


def two_halves(wavefunction, left_env, right_env, mpo_mask, block_size, route_owner, route_block):
    blocks, states, _ = wavefunction.shape
    share = states // 2
    rows = share // ROW_GROUPS
    width = states // COL_PARTS
    span = width // PHASES
    peers = lax.axis_size("sector")
    total = blocks * PIECES
    place = jnp.stack([lax.axis_index("mpo"), lax.axis_index("sector")]).astype(jnp.int32)
    owners, targets = route_owner.reshape(-1), route_block.reshape(-1)
    swap = [(0, 1), (1, 0)]

    src, info = pl.pallas_call(
        functools.partial(route_kernel, peers, blocks, rows, width),
        in_specs=[SMEM] * 4,
        out_specs=[SMEM, SMEM],
        out_shape=[jax.ShapeDtypeStruct((LANES,), jnp.int32)] * 2,
        scratch_shapes=[pltpu.SMEM((peers,), jnp.int32)],
        name="route",
    )(place, owners, targets, block_size)
    spill_src = src[peers * SLOTS : peers * SLOTS + SPILL]
    told = lax.ppermute(src, "mpo", swap)
    more = jnp.maximum(src[LANES - 1], told[LANES - 1])
    lane = lax.broadcasted_iota(jnp.int32, (INFO, LANES), 1)
    table = jnp.where(lane == LANES - 1, more, info[None, :]).astype(jnp.bfloat16)

    own, send, other = [], [], []
    for phase in range(PHASES):
        mine, theirs = terms(place, block_size, mpo_mask[0], wavefunction, left_env[0], right_env[0], phase, share)
        own.append(mine.reshape(total * rows, span))
        send.append(theirs.reshape(total * rows, span))
        other.append(lax.ppermute(send[-1], "mpo", swap))

    asked = told[peers * SLOTS : peers * SLOTS + SPILL]
    spill_other = lax.ppermute(pick(asked, send, rows), "mpo", swap)
    spill_own = pick(spill_src, own, rows)
    chunk = PHASES * SPILL * rows + INFO
    spilled = pl.pallas_call(
        spill_kernel,
        in_specs=[VMEM] * 3,
        out_specs=VMEM,
        out_shape=jax.ShapeDtypeStruct((chunk, LANES), jnp.bfloat16),
        compiler_params=params(16),
        name="spill",
    )(spill_own, spill_other, table)

    def across(x, apart):
        return lax.ppermute(x, "sector", [(i, i ^ apart) for i in range(peers)])

    near = jnp.concatenate([spilled] + [across(spilled, apart) for apart in range(4, peers, 4)], axis=0)
    beside = across(near, 2)
    sets = [near, beside, across(near, 1), across(beside, 1)]
    tables = jnp.concatenate([s.reshape(peers // 4, chunk, LANES)[:, chunk - INFO] for s in sets], axis=0).astype(jnp.int32)

    arrived = []
    for phase in range(PHASES):
        packed = pack(src, own[phase], other[phase], rows, peers * SLOTS)
        packed = packed.reshape(peers, SLOTS * rows, span)
        landed = lax.all_to_all(packed, "sector", split_axis=0, concat_axis=0, tiled=True)
        arrived.append(landed.reshape(peers * SLOTS * rows, span))

    done, later = pl.pallas_call(
        functools.partial(early_kernel, rows, peers),
        in_specs=[SMEM, SMEM] + [VMEM] * 5,
        out_specs=[VMEM, VMEM],
        out_shape=[
            jax.ShapeDtypeStruct((total * rows, span), jnp.bfloat16),
            jax.ShapeDtypeStruct((total * rows, span), jnp.float32),
        ],
        scratch_shapes=[pltpu.VMEM((total * rows, span), jnp.float32)],
        compiler_params=params(32),
        name="early",
    )(place, tables, arrived[0], *sets)

    def fast(place, tables, landed, done, later, *_):
        return pl.pallas_call(
            functools.partial(late_kernel, rows, peers),
            in_specs=[SMEM, SMEM] + [VMEM] * 3,
            out_specs=VMEM,
            out_shape=jax.ShapeDtypeStruct((blocks, share, states), jnp.bfloat16),
            scratch_shapes=[pltpu.VMEM((total * rows, span), jnp.float32)],
            compiler_params=params(32),
            name="late",
        )(place, tables, landed, done, later)

    def slow(place, tables, landed, done, later, own, other):
        whole = [(a.astype(jnp.float32) + b.astype(jnp.float32)).astype(jnp.bfloat16) for a, b in zip(own, other)]
        whole = [w.reshape(blocks, COL_PARTS, share, span) for w in whole]
        sigma = jnp.stack(whole, axis=3).transpose(2, 0, 1, 3, 4).reshape(share, blocks, states)
        return exchange_all(sigma, route_owner, route_block)

    enough = jnp.max(tables[:, LANES - 1]) <= 0
    return lax.cond(enough, fast, slow, place, tables, arrived[1], done, later, tuple(own), tuple(other))


def solution(mesh):
    placed = (
        P("sector", None, None),
        P("mpo", "sector", None, None),
        P("mpo", "sector", None, None),
        P("mpo", "sector"),
        P("sector"),
        P("mpo", "sector", None),
        P("mpo", "sector", None),
    )

    def per_device(wavefunction, *rest):
        states = wavefunction.shape[1]
        peers = mesh.shape["sector"]
        fits = (
            mesh.shape["mpo"] == 2
            and peers >= 8
            and peers & (peers - 1) == 0
            and states // COL_PARTS == PHASES * LANES
            and states // (2 * ROW_GROUPS) % 16 == 0
            and peers * SLOTS + 2 * SPILL < LANES
        )
        return (two_halves if fits else general)(wavefunction, *rest)

    return jax.shard_map(per_device, mesh=mesh, in_specs=placed, out_specs=P("sector", "mpo", None), check_vma=False)
```

```python
import functools

import jax
import jax.numpy as jnp
from jax import lax
from jax.experimental import pallas as pl
from jax.experimental.pallas import tpu as pltpu
from jax.sharding import PartitionSpec as P

ROW_GROUPS = 4
COL_PARTS = 2
PIECES = 8
SLOTS = 2
SPILL = 3
SPILL_BLOCKS = 2
INFO = 16
TABLE = 256

VMEM = pl.BlockSpec(memory_space=pltpu.VMEM)
SMEM = pl.BlockSpec(memory_space=pltpu.SMEM)
ANY = pl.BlockSpec(memory_space=pl.ANY)
HBM = pl.BlockSpec(memory_space=pltpu.HBM)


def params(mib):
    return pltpu.CompilerParams(vmem_limit_bytes=mib * 2**20)


def exchange_all(sigma_share, route_owner, route_block):
    row_count, block_count, states = sigma_share.shape
    group_rows = row_count // ROW_GROUPS
    width_part = states // COL_PARTS
    pieces = sigma_share.reshape(ROW_GROUPS, group_rows, block_count, COL_PARTS, width_part)
    pieces = pieces.transpose(2, 0, 3, 1, 4).reshape(block_count * PIECES, group_rows * width_part)
    owners = route_owner[0].reshape(-1)
    target_code = (route_block[0] * PIECES + jnp.arange(PIECES, dtype=jnp.int32)[None, :]).reshape(-1)
    peer_count = lax.axis_size("sector")
    capacity = min(block_count, max(2, (2 * block_count * PIECES + peer_count - 1) // peer_count))
    is_owner = (owners[:, None] == jnp.arange(peer_count, dtype=jnp.int32)[None, :]).astype(jnp.int32)
    before = jnp.cumsum(is_owner, axis=0) - is_owner
    position = jnp.sum(before * is_owner, axis=1)
    destination = owners * capacity + position
    slot_ids = jnp.arange(peer_count * capacity, dtype=jnp.int32)
    placing = slot_ids[:, None] == destination[None, :]
    send_data = jnp.dot(placing.astype(jnp.bfloat16), pieces, preferred_element_type=jnp.float32).astype(jnp.bfloat16)
    send_data = send_data.reshape(peer_count, capacity, group_rows * width_part)
    send_code = (jnp.sum(placing.astype(jnp.int32) * (target_code + 1)[None, :], axis=1) - 1).reshape(peer_count, capacity)
    arrived_data, arrived_code = (
        lax.all_to_all(send_data, "sector", split_axis=0, concat_axis=0, tiled=True),
        lax.all_to_all(send_code, "sector", split_axis=0, concat_axis=0, tiled=True),
    )
    arrived_data = arrived_data.reshape(peer_count * capacity, group_rows * width_part)
    arrived_code = arrived_code.reshape(-1)
    targets = jnp.arange(block_count * PIECES, dtype=jnp.int32)
    collect = (arrived_code[None, :] == targets[:, None]).astype(jnp.bfloat16)
    landed = jnp.dot(collect, arrived_data, preferred_element_type=jnp.float32).astype(jnp.bfloat16)
    landed = landed.reshape(block_count, ROW_GROUPS, COL_PARTS, group_rows, width_part)
    return landed.transpose(0, 1, 3, 2, 4).reshape(block_count, row_count, states)


def general(wavefunction, left_env, right_env, mpo_mask, block_size, route_owner, route_block):
    states = wavefunction.shape[1]
    row_count = states // lax.axis_size("mpo")
    positions = jnp.arange(states, dtype=jnp.int32)
    live_cols = positions[None, :] < block_size[:, None]
    live_mask = live_cols[:, :, None] & live_cols[:, None, :]
    masked = jnp.where(live_mask, wavefunction, jnp.zeros_like(wavefunction))
    right_part = jnp.einsum("bij,bkj->bik", masked, right_env[0], preferred_element_type=jnp.float32).astype(jnp.bfloat16)
    factor = mpo_mask[0].astype(jnp.float32)
    product = jnp.einsum("bij,bjk->ibk", left_env[0], right_part, preferred_element_type=jnp.float32)
    row_share = lax.psum_scatter(
        (product * factor[None, :, None]).astype(jnp.bfloat16), "mpo", scatter_dimension=0, tiled=True
    ).astype(jnp.float32)
    global_rows = lax.axis_index("mpo") * row_count + jnp.arange(row_count, dtype=jnp.int32)
    live_rows = global_rows[:, None] < block_size[None, :]
    share_mask = live_rows[:, :, None] & live_cols[None, :, :]
    sigma_share = jnp.where(share_mask, row_share, jnp.zeros_like(row_share)).astype(jnp.bfloat16)
    return exchange_all(sigma_share, route_owner, route_block)


def route_kernel(peers, blocks, group_rows, width, owner_ref, block_ref, size_ref, behind_ref, sent_ref, info_ref, count):
    first_row = lax.axis_index("mpo") * (ROW_GROUPS * group_rows)
    spill_at = peers * SLOTS
    for i in range(spill_at + 2 * SPILL):
        info_ref[i] = -1
    for i in range(SPILL):
        sent_ref[blocks * PIECES + i] = -1
    for i in range(peers):
        count[i] = 0

    nowhere = TABLE - 2

    def one(step, spilled):
        b, k = blocks - 1 - step // PIECES, step % PIECES
        i = b * PIECES + k
        g, c = k // COL_PARTS, k % COL_PARTS
        size = size_ref[b]
        live = (first_row + g * group_rows < size) & (c * width < size)
        owner = owner_ref[0, b, k]
        pos = count[owner]
        code = block_ref[0, b, k] * PIECES + k
        direct = live & (pos < SLOTS)
        kept = live & (pos >= SLOTS) & (spilled < SPILL)
        sent_ref[i] = jnp.where(direct, owner * SLOTS + pos, -1)
        info_ref[jnp.where(direct, owner * SLOTS + pos, nowhere)] = code
        count[owner] = pos + direct.astype(jnp.int32)
        sent_ref[jnp.where(kept, blocks * PIECES + spilled, nowhere)] = i
        info_ref[jnp.where(kept, spill_at + spilled, nowhere)] = owner
        info_ref[jnp.where(kept, spill_at + SPILL + spilled, nowhere)] = code
        return spilled + (live & (pos >= SLOTS)).astype(jnp.int32)

    spilled = lax.fori_loop(0, blocks * PIECES, one, 0, unroll=PIECES)
    sent_ref[TABLE - 1] = (spilled > SPILL).astype(jnp.int32)


def term_kernel(first, size_ref, mask_ref, wave_ref, left_ref, right_ref, *refs):
    own_ref, send_ref, wave, left, right, own, send, come, go = refs[-9:]
    count, states, _ = wave.shape
    share = states // 2
    rows, width = share // ROW_GROUPS, states // COL_PARTS
    mine = lax.axis_index("mpo").astype(jnp.int32)
    arrive = []
    for n in range(count):
        arrive.append(
            [
                pltpu.make_async_copy(source.at[first + n], target.at[n], come.at[n, i])
                for i, (source, target) in enumerate(((wave_ref, wave), (right_ref, right), (left_ref, left)))
            ]
        )
        for copy in arrive[-1]:
            copy.start()
    row = lax.broadcasted_iota(jnp.int32, (states, states), 0)
    col = lax.broadcasted_iota(jnp.int32, (states, states), 1)
    leave = []
    for n in range(count):
        size = size_ref[first + n]
        active = mask_ref[0, first + n] != 0
        arrive[n][0].wait()
        masked = jnp.where((row < size) & (col < size), wave[n], jnp.zeros_like(wave[n]))
        arrive[n][1].wait()
        part = lax.dot_general(masked, right[n], (((1,), (1,)), ((), ())), preferred_element_type=jnp.float32)
        part = part.astype(jnp.bfloat16)
        arrive[n][2].wait()
        for which, (target, out_ref, half) in enumerate(((send, send_ref, 1 - mine), (own, own_ref, mine))):
            start = pl.multiple_of(half * share, share)
            product = jnp.dot(left[n, pl.ds(start, share), :], part, preferred_element_type=jnp.float32)
            keep = (row[:share] + start < size) & (col[:share] < size) & active
            product = jnp.where(keep, product, 0.0).astype(jnp.bfloat16)
            for k in range(PIECES):
                g, c = k // COL_PARTS, k % COL_PARTS
                target[n, k * rows : (k + 1) * rows, :] = product[g * rows : (g + 1) * rows, c * width : (c + 1) * width]
            to = pl.ds(n * PIECES * rows, PIECES * rows)
            leave.append(pltpu.make_async_copy(target.at[n], out_ref.at[to], go.at[n, which]))
            leave[-1].start()
    for copy in leave:
        copy.wait()


def terms(first, count, sizes, mask, wave, left, right, behind):
    states = wave.shape[1]
    rows, width = states // 2 * COL_PARTS, states // COL_PARTS
    out = jax.ShapeDtypeStruct((count * rows, width), jnp.bfloat16)
    return pl.pallas_call(
        functools.partial(term_kernel, first),
        in_specs=[SMEM] * 2 + [HBM] * 3 + [ANY] * len(behind),
        out_specs=[HBM, HBM],
        out_shape=[out, out],
        scratch_shapes=[pltpu.VMEM((count, states, states), jnp.bfloat16)] * 3
        + [pltpu.VMEM((count, rows, width), jnp.bfloat16)] * 2
        + [pltpu.SemaphoreType.DMA((count, 3)), pltpu.SemaphoreType.DMA((count, 2))],
        compiler_params=params(63),
        name="terms",
    )(sizes, mask, wave, left, right, *behind)


def add(a, b):
    return (a.astype(jnp.float32) + b.astype(jnp.float32)).astype(jnp.bfloat16)


def fetch_spill(rows, blocks, sent_ref, sources, target, sems):
    for j in range(SPILL):
        index = sent_ref[blocks * PIECES + j]
        for b in range(SPILL_BLOCKS):

            def copy(b=b, j=j, index=index):
                at = pl.ds(pl.multiple_of((index - b * PIECES) * rows, rows), rows)
                return pltpu.make_async_copy(sources[b].at[at], target.at[pl.ds(j * rows, rows)], sems.at[j])

            yield (index >= b * PIECES) & (index < (b + 1) * PIECES), copy


def run_copies(copies):
    copies = list(copies)
    for step in ("start", "wait"):
        for there, copy in copies:

            @pl.when(there)
            def _(copy=copy, step=step):
                getattr(copy(), step)()


def spill_kernel(rows, blocks, sent_ref, info_ref, *refs):
    own_refs, other_refs = refs[:SPILL_BLOCKS], refs[SPILL_BLOCKS : 2 * SPILL_BLOCKS]
    out_ref, own, other, own_sems, other_sems = refs[2 * SPILL_BLOCKS + 1 :]
    run_copies(
        [*fetch_spill(rows, blocks, sent_ref, own_refs, own, own_sems), *fetch_spill(rows, blocks, sent_ref, other_refs, other, other_sems)]
    )
    out_ref[: SPILL * rows, :] = add(own[...], other[...])
    lane = lax.broadcasted_iota(jnp.int32, (INFO, TABLE), 1)
    table = jnp.where(lane == TABLE - 1, sent_ref[TABLE - 1], info_ref[...])
    out_ref[SPILL * rows :, :] = table.astype(jnp.float32).astype(jnp.bfloat16)


def join_kernel(count, *refs):
    out_ref, sems = refs[-2:]
    copies = []
    for i, ref in enumerate(refs[:count]):
        copies.append(pltpu.make_async_copy(ref, out_ref.at[pl.ds(i * ref.shape[0], ref.shape[0])], sems.at[i]))
        copies[-1].start()
    for copy in copies:
        copy.wait()


def join(behind, *parts):
    rows, width = parts[0].shape
    return pl.pallas_call(
        functools.partial(join_kernel, len(parts)),
        in_specs=[HBM] * len(parts) + [ANY] * len(behind),
        out_specs=HBM,
        out_shape=jax.ShapeDtypeStruct((len(parts) * rows, width), jnp.bfloat16),
        scratch_shapes=[pltpu.SemaphoreType.DMA((len(parts),))],
        compiler_params=params(63),
        name="join",
    )(*parts, *behind)


def pack_kernel(first, rows, pairs, sent_ref, *refs):
    own_refs, other_refs = refs[:pairs], refs[pairs : 2 * pairs]
    out_ref, stage, sems = refs[-3:]
    done = 0
    copies = []
    for own_ref, other_ref in zip(own_refs, other_refs):
        count = own_ref.shape[0] // rows
        stage[done * rows : (done + count) * rows, :] = add(own_ref[...], other_ref[...])
        for k in range(done, done + count):
            slot = sent_ref[first * PIECES + k]

            def copy(k=k, slot=slot):
                to = pl.ds(pl.multiple_of(slot * rows, rows), rows)
                return pltpu.make_async_copy(stage.at[pl.ds(k * rows, rows)], out_ref.at[to], sems.at[k])

            copies.append((slot >= 0, copy))

            @pl.when(slot >= 0)
            def _(copy=copy):
                copy().start()

        done += count
    for there, copy in copies:

        @pl.when(there)
        def _(copy=copy):
            copy().wait()


def pack(first, sent, own, other, packed, rows, slots, behind):
    total, width = sum(x.shape[0] for x in own), own[0].shape[1]
    before = [] if packed is None else [packed]
    pairs = len(own)
    return pl.pallas_call(
        functools.partial(pack_kernel, first, rows, pairs),
        in_specs=[SMEM] + [VMEM] * (2 * pairs) + [HBM] * len(before) + [ANY] * len(behind),
        out_specs=HBM,
        out_shape=jax.ShapeDtypeStruct((slots * rows, width), jnp.bfloat16),
        scratch_shapes=[pltpu.VMEM((total, width), jnp.bfloat16), pltpu.SemaphoreType.DMA((total // rows,))],
        input_output_aliases={1 + 2 * pairs: 0} if before else {},
        compiler_params=params(63),
        name="pack",
    )(sent, *own, *other, *before, *behind)


def list_kernel(rows, peers, blocks, *refs):
    sets, (order_ref, begin_ref, more_ref, lines, values, table, codes, count, sems) = refs[:4], refs[4:]
    me = lax.axis_index("sector")
    quarter = peers // 4
    chunk = SPILL * rows + INFO
    slots, targets = peers * SLOTS, blocks * PIECES
    copies = []
    for which, ref in enumerate(sets):
        for z in range(quarter):
            i = which * quarter + z
            copies.append(pltpu.make_async_copy(ref.at[pl.ds((z + 1) * chunk - INFO, INFO)], lines.at[i], sems.at[i]))
            copies[-1].start()
    for i in range(targets):
        count[i] = 0
    for i, copy in enumerate(copies):
        copy.wait()
        values[i : i + 1, :] = lines[i].astype(jnp.float32).astype(jnp.int32)[:1, :]
    copy = pltpu.make_async_copy(values, table, sems.at[peers])
    copy.start()
    copy.wait()

    def note(i, code):
        codes[i] = code

        @pl.when(code >= 0)
        def _():
            count[code] += 1

    def source(j, more):
        apart = j ^ me
        line = ((apart & 1) * 2 + ((apart >> 1) & 1)) * quarter + (apart >> 2)
        for slot in range(SLOTS):
            note(j * SLOTS + slot, table[line, me * SLOTS + slot])
        for i in range(SPILL):
            owner = table[j, slots + i]
            note(slots + j * SPILL + i, jnp.where(owner == me, table[j, slots + SPILL + i], -1))
        return jnp.maximum(more, table[j, TABLE - 1])

    more_ref[0] = lax.fori_loop(0, peers, source, 0)

    def total(t, before):
        begin_ref[t] = before
        after = before + count[t]
        count[t] = before
        return after

    begin_ref[targets] = lax.fori_loop(0, targets, total, 0)

    def put(i, _):
        code = codes[i]

        @pl.when(code >= 0)
        def _():
            place = count[code]
            order_ref[place] = i
            count[code] = place + 1

        return 0

    lax.fori_loop(0, slots + peers * SPILL, put, 0)


def land_kernel(rows, peers, order_ref, begin_ref, arrived_ref, *refs):
    sets, (out_ref, held, stage, sems, out_sems) = refs[:4], refs[4:]
    quarter = peers // 4
    chunk = SPILL * rows + INFO
    slots = peers * SLOTS
    blocks, share, states = stage.shape
    width = states // COL_PARTS

    def at(start, unit=rows):
        return pl.ds(pl.multiple_of(start, unit), rows)

    def fetch(i, ref, start):
        return pltpu.make_async_copy(ref.at[at(start, 16)], held.at[at(i * rows)], sems.at[i])

    def begin(n, _):
        i = order_ref[n]

        @pl.when(i < slots)
        def _():
            fetch(i, arrived_ref, i * rows).start()

        @pl.when(i >= slots)
        def _():
            source, j = (i - slots) // SPILL, (i - slots) % SPILL
            for which in range(4):

                @pl.when(source // quarter == which)
                def _(which=which):
                    fetch(i, sets[which], source % quarter * chunk + j * rows).start()

        return 0

    lax.fori_loop(0, begin_ref[blocks * PIECES], begin, 0)

    copies = []
    for t in range(blocks):
        for k in range(PIECES):
            g, c = k // COL_PARTS, k % COL_PARTS
            first, last = begin_ref[t * PIECES + k], begin_ref[t * PIECES + k + 1]

            def more(n, total):
                i = order_ref[n]
                fetch(i, arrived_ref, 0).wait()
                return total + held[at(i * rows), :].astype(jnp.float32)

            total = lax.fori_loop(first, last, more, jnp.zeros((rows, width), jnp.float32))
            stage[t, g * rows : (g + 1) * rows, c * width : (c + 1) * width] = total.astype(jnp.bfloat16)
        copies.append(pltpu.make_async_copy(stage.at[t], out_ref.at[t], out_sems.at[t]))
        copies[-1].start()
    for copy in copies:
        copy.wait()


def two_halves(wavefunction, left_env, right_env, mpo_mask, block_size, route_owner, route_block):
    blocks, states, _ = wavefunction.shape
    share = states // 2
    rows = share // ROW_GROUPS
    width = states // COL_PARTS
    peers = lax.axis_size("sector")
    chunk = SPILL * rows + INFO

    def bf16(*shape):
        return jax.ShapeDtypeStruct(shape, jnp.bfloat16)

    def int32(*shape):
        return jax.ShapeDtypeStruct(shape, jnp.int32)

    def swap(x):
        return lax.ppermute(x, "mpo", [(0, 1), (1, 0)])

    def across(x, apart):
        return lax.ppermute(x, "sector", [(i, i ^ apart) for i in range(peers)])

    own, send, other = [], [], []

    def run(first, count, behind):
        mine, theirs = terms(first, count, block_size, mpo_mask, wavefunction, left_env[0], right_env[0], behind)
        own.append(mine)
        send.append(theirs)
        other.append(swap(theirs))

    for b in range(SPILL_BLOCKS):
        run(b, 1, send[-1:])
    run(SPILL_BLOCKS, blocks - SPILL_BLOCKS, send[-1:])
    sent, info = pl.pallas_call(
        functools.partial(route_kernel, peers, blocks, rows, width),
        in_specs=[SMEM] * 3 + [ANY],
        out_specs=[SMEM, SMEM],
        out_shape=[int32(TABLE)] * 2,
        scratch_shapes=[pltpu.SMEM((peers,), jnp.int32)],
        name="route",
    )(route_owner, route_block, block_size, send[-1])
    spilled = pl.pallas_call(
        functools.partial(spill_kernel, rows, blocks),
        in_specs=[SMEM, VMEM] + [HBM] * (2 * SPILL_BLOCKS) + [ANY],
        out_specs=VMEM,
        out_shape=bf16(chunk, width),
        scratch_shapes=[pltpu.VMEM((SPILL * rows, width), jnp.bfloat16)] * 2 + [pltpu.SemaphoreType.DMA((SPILL,))] * 2,
        compiler_params=params(63),
        name="spill",
    )(sent, info.reshape(1, TABLE), *own[:SPILL_BLOCKS], *other[:SPILL_BLOCKS], send[-1])
    packed = pack(0, sent, own[:SPILL_BLOCKS], other[:SPILL_BLOCKS], None, rows, peers * SLOTS, [])
    near = join([packed], spilled, *[across(spilled, apart) for apart in range(4, peers, 4)])
    beside = across(near, 2)
    sets = [near, beside, across(near, 1), across(beside, 1)]
    packed = pack(SPILL_BLOCKS, sent, own[SPILL_BLOCKS:], other[SPILL_BLOCKS:], packed, rows, peers * SLOTS, [near])
    arrived = lax.all_to_all(packed.reshape(peers, SLOTS * rows, width), "sector", split_axis=0, concat_axis=0, tiled=True)
    arrived = arrived.reshape(peers * SLOTS * rows, width)

    pieces = peers * (SLOTS + SPILL)
    order, begin, more = pl.pallas_call(
        functools.partial(list_kernel, rows, peers, blocks),
        in_specs=[HBM] * 4,
        out_specs=[SMEM] * 3,
        out_shape=[int32(pieces), int32(blocks * PIECES + 1), int32(1)],
        scratch_shapes=[
            pltpu.VMEM((peers, INFO, TABLE), jnp.bfloat16),
            pltpu.VMEM((peers, TABLE), jnp.int32),
            pltpu.SMEM((peers, TABLE), jnp.int32),
            pltpu.SMEM((pieces,), jnp.int32),
            pltpu.SMEM((blocks * PIECES,), jnp.int32),
            pltpu.SemaphoreType.DMA((peers + 1,)),
        ],
        compiler_params=params(63),
        cost_estimate=pl.CostEstimate(flops=16000000000, bytes_accessed=0, transcendentals=0),
        name="list",
    )(*sets)

    def fast(order, begin, arrived, sets, *_):
        return pl.pallas_call(
            functools.partial(land_kernel, rows, peers),
            in_specs=[SMEM, SMEM] + [HBM] * 5,
            out_specs=HBM,
            out_shape=bf16(blocks, share, states),
            scratch_shapes=[
                pltpu.VMEM((pieces * rows, width), jnp.bfloat16),
                pltpu.VMEM((blocks, share, states), jnp.bfloat16),
                pltpu.SemaphoreType.DMA((pieces,)),
                pltpu.SemaphoreType.DMA((blocks,)),
            ],
            compiler_params=params(63),
            name="land",
        )(order, begin, arrived, *sets)

    def slow(order, begin, arrived, sets, own, other):
        sums = jnp.concatenate([add(a, b) for a, b in zip(own, other)], axis=0)
        sums = sums.reshape(blocks, ROW_GROUPS, COL_PARTS, rows, width).transpose(1, 3, 0, 2, 4)
        return exchange_all(sums.reshape(share, blocks, states), route_owner, route_block)

    more = jnp.maximum(more, swap(more))
    return lax.cond(more[0] <= 0, fast, slow, order, begin, arrived, tuple(sets), tuple(own), tuple(other))


def solution(mesh):
    placed = (
        P("sector", None, None),
        P("mpo", "sector", None, None),
        P("mpo", "sector", None, None),
        P("mpo", "sector"),
        P("sector"),
        P("mpo", "sector", None),
        P("mpo", "sector", None),
    )

    def per_device(wavefunction, *rest):
        states = wavefunction.shape[1]
        peers = mesh.shape["sector"]
        fits = (
            mesh.shape["mpo"] == 2
            and peers >= 8
            and peers & (peers - 1) == 0
            and wavefunction.shape[0] == SLOTS + SPILL_BLOCKS
            and states // COL_PARTS == TABLE
            and states // (2 * ROW_GROUPS) % 16 == 0
            and peers * SLOTS + 2 * SPILL < TABLE
        )
        return (two_halves if fits else general)(wavefunction, *rest)

    return jax.shard_map(per_device, mesh=mesh, in_specs=placed, out_specs=P("sector", "mpo", None), check_vma=False)
```

```python
import functools

import jax
import jax.numpy as jnp
from jax import lax
from jax.experimental import pallas as pl
from jax.experimental.pallas import tpu as pltpu
from jax.sharding import PartitionSpec as P

ROW_GROUPS = 4
COL_PARTS = 2
PIECES = 8
SLOTS = 2
SPILL = 3
SPILL_BLOCKS = 2
INFO = 16
TABLE = 256

VMEM = pl.BlockSpec(memory_space=pltpu.VMEM)
SMEM = pl.BlockSpec(memory_space=pltpu.SMEM)
ANY = pl.BlockSpec(memory_space=pl.ANY)
HBM = pl.BlockSpec(memory_space=pltpu.HBM)


def params(mib):
    return pltpu.CompilerParams(vmem_limit_bytes=mib * 2**20)


def exchange_all(sigma_share, route_owner, route_block):
    row_count, block_count, states = sigma_share.shape
    group_rows = row_count // ROW_GROUPS
    width_part = states // COL_PARTS
    pieces = sigma_share.reshape(ROW_GROUPS, group_rows, block_count, COL_PARTS, width_part)
    pieces = pieces.transpose(2, 0, 3, 1, 4).reshape(block_count * PIECES, group_rows * width_part)
    owners = route_owner[0].reshape(-1)
    target_code = (route_block[0] * PIECES + jnp.arange(PIECES, dtype=jnp.int32)[None, :]).reshape(-1)
    peer_count = lax.axis_size("sector")
    capacity = min(block_count, max(2, (2 * block_count * PIECES + peer_count - 1) // peer_count))
    is_owner = (owners[:, None] == jnp.arange(peer_count, dtype=jnp.int32)[None, :]).astype(jnp.int32)
    before = jnp.cumsum(is_owner, axis=0) - is_owner
    position = jnp.sum(before * is_owner, axis=1)
    destination = owners * capacity + position
    slot_ids = jnp.arange(peer_count * capacity, dtype=jnp.int32)
    placing = slot_ids[:, None] == destination[None, :]
    send_data = jnp.dot(placing.astype(jnp.bfloat16), pieces, preferred_element_type=jnp.float32).astype(jnp.bfloat16)
    send_data = send_data.reshape(peer_count, capacity, group_rows * width_part)
    send_code = (jnp.sum(placing.astype(jnp.int32) * (target_code + 1)[None, :], axis=1) - 1).reshape(peer_count, capacity)
    arrived_data, arrived_code = (
        lax.all_to_all(send_data, "sector", split_axis=0, concat_axis=0, tiled=True),
        lax.all_to_all(send_code, "sector", split_axis=0, concat_axis=0, tiled=True),
    )
    arrived_data = arrived_data.reshape(peer_count * capacity, group_rows * width_part)
    arrived_code = arrived_code.reshape(-1)
    targets = jnp.arange(block_count * PIECES, dtype=jnp.int32)
    collect = (arrived_code[None, :] == targets[:, None]).astype(jnp.bfloat16)
    landed = jnp.dot(collect, arrived_data, preferred_element_type=jnp.float32).astype(jnp.bfloat16)
    landed = landed.reshape(block_count, ROW_GROUPS, COL_PARTS, group_rows, width_part)
    return landed.transpose(0, 1, 3, 2, 4).reshape(block_count, row_count, states)


def general(wavefunction, left_env, right_env, mpo_mask, block_size, route_owner, route_block):
    states = wavefunction.shape[1]
    row_count = states // lax.axis_size("mpo")
    positions = jnp.arange(states, dtype=jnp.int32)
    live_cols = positions[None, :] < block_size[:, None]
    live_mask = live_cols[:, :, None] & live_cols[:, None, :]
    masked = jnp.where(live_mask, wavefunction, jnp.zeros_like(wavefunction))
    right_part = jnp.einsum("bij,bkj->bik", masked, right_env[0], preferred_element_type=jnp.float32).astype(jnp.bfloat16)
    factor = mpo_mask[0].astype(jnp.float32)
    product = jnp.einsum("bij,bjk->ibk", left_env[0], right_part, preferred_element_type=jnp.float32)
    row_share = lax.psum_scatter(
        (product * factor[None, :, None]).astype(jnp.bfloat16), "mpo", scatter_dimension=0, tiled=True
    ).astype(jnp.float32)
    global_rows = lax.axis_index("mpo") * row_count + jnp.arange(row_count, dtype=jnp.int32)
    live_rows = global_rows[:, None] < block_size[None, :]
    share_mask = live_rows[:, :, None] & live_cols[None, :, :]
    sigma_share = jnp.where(share_mask, row_share, jnp.zeros_like(row_share)).astype(jnp.bfloat16)
    return exchange_all(sigma_share, route_owner, route_block)


def route(peers, blocks, group_rows, width, owner_ref, block_ref, size_ref, sent_ref, info_ref, count):
    first_row = lax.axis_index("mpo") * (ROW_GROUPS * group_rows)
    spill_at = peers * SLOTS
    for i in range(spill_at + 2 * SPILL):
        info_ref[i] = -1
    for i in range(SPILL):
        sent_ref[blocks * PIECES + i] = -1
    for i in range(peers):
        count[i] = 0

    nowhere = TABLE - 2

    def one(step, spilled):
        b, k = blocks - 1 - step // PIECES, step % PIECES
        i = b * PIECES + k
        g, c = k // COL_PARTS, k % COL_PARTS
        size = size_ref[b]
        live = (first_row + g * group_rows < size) & (c * width < size)
        owner = owner_ref[0, b, k]
        pos = count[owner]
        code = block_ref[0, b, k] * PIECES + k
        direct = live & (pos < SLOTS)
        kept = live & (pos >= SLOTS) & (spilled < SPILL)
        sent_ref[i] = jnp.where(direct, owner * SLOTS + pos, -1)
        info_ref[jnp.where(direct, owner * SLOTS + pos, nowhere)] = code
        count[owner] = pos + direct.astype(jnp.int32)
        sent_ref[jnp.where(kept, blocks * PIECES + spilled, nowhere)] = i
        info_ref[jnp.where(kept, spill_at + spilled, nowhere)] = owner
        info_ref[jnp.where(kept, spill_at + SPILL + spilled, nowhere)] = code
        return spilled + (live & (pos >= SLOTS)).astype(jnp.int32)

    spilled = lax.fori_loop(0, blocks * PIECES, one, 0, unroll=PIECES)
    sent_ref[TABLE - 1] = (spilled > SPILL).astype(jnp.int32)


def term_kernel(first, plan, size_ref, mask_ref, wave_ref, left_ref, right_ref, *refs):
    tables = ()
    if plan:
        tables = (*refs[:2], size_ref, *refs[-11:-9], refs[-1])
        refs = refs[2:-11] + refs[-9:-1]
    wave, left, right, own, send, mark, come, go = refs[-8:]
    results = refs[-8 - 2 * wave.shape[0] : -8]
    count, states, _ = wave.shape
    share = states // 2
    rows, width = share // ROW_GROUPS, states // COL_PARTS
    mine = lax.axis_index("mpo").astype(jnp.int32)
    arrive = []
    for n in range(count):
        arrive.append(
            [
                pltpu.make_async_copy(source.at[first + n], target.at[n], come.at[n, i])
                for i, (source, target) in enumerate(((wave_ref, wave), (right_ref, right), (left_ref, left)))
            ]
        )
        for copy in arrive[-1]:
            copy.start()
    leave = []
    if plan:
        route(*plan, *tables)
        mark[...] = jnp.full(mark.shape, tables[3][TABLE - 1], jnp.int32).astype(jnp.float32).astype(jnp.bfloat16)
        leave.append(pltpu.make_async_copy(mark, results[2 * count - 1].at[pl.ds(PIECES * rows, INFO)], go.at[count, 0]))
        leave[-1].start()
    row = lax.broadcasted_iota(jnp.int32, (states, states), 0)
    col = lax.broadcasted_iota(jnp.int32, (states, states), 1)
    for n in range(count):
        size = size_ref[first + n]
        active = mask_ref[0, first + n] != 0
        arrive[n][0].wait()
        masked = jnp.where((row < size) & (col < size), wave[n], jnp.zeros_like(wave[n]))
        arrive[n][1].wait()
        part = lax.dot_general(masked, right[n], (((1,), (1,)), ((), ())), preferred_element_type=jnp.float32)
        part = part.astype(jnp.bfloat16)
        arrive[n][2].wait()
        for which, (target, out_ref, half) in enumerate(((send, results[2 * n + 1], 1 - mine), (own, results[2 * n], mine))):
            start = pl.multiple_of(half * share, share)
            product = jnp.dot(left[n, pl.ds(start, share), :], part, preferred_element_type=jnp.float32)
            keep = (row[:share] + start < size) & (col[:share] < size) & active
            product = jnp.where(keep, product, 0.0).astype(jnp.bfloat16)
            for k in range(PIECES):
                g, c = k // COL_PARTS, k % COL_PARTS
                target[n, k * rows : (k + 1) * rows, :] = product[g * rows : (g + 1) * rows, c * width : (c + 1) * width]
            leave.append(pltpu.make_async_copy(target.at[n], out_ref.at[pl.ds(0, PIECES * rows)], go.at[n, which]))
            leave[-1].start()
    for copy in leave:
        copy.wait()


def terms(first, count, sizes, mask, wave, left, right, plan, behind):
    blocks, states, _ = wave.shape
    group_rows, width = states // 2 // ROW_GROUPS, states // COL_PARTS
    rows = PIECES * group_rows
    out = jax.ShapeDtypeStruct((rows, width), jnp.bfloat16)
    longer = jax.ShapeDtypeStruct((rows + INFO, width), jnp.bfloat16)
    table = jax.ShapeDtypeStruct((TABLE,), jnp.int32)
    peers = lax.axis_size("sector")
    scratch = [pltpu.VMEM((count, states, states), jnp.bfloat16)] * 3 + [pltpu.VMEM((count, rows, width), jnp.bfloat16)] * 2
    scratch += [pltpu.VMEM((INFO, width), jnp.bfloat16), pltpu.SemaphoreType.DMA((count, 3)), pltpu.SemaphoreType.DMA((count + 1, 2))]
    if plan:
        scratch += [pltpu.SMEM((peers,), jnp.int32)]
    return pl.pallas_call(
        functools.partial(term_kernel, first, (peers, blocks, group_rows, width) if plan else None),
        in_specs=[SMEM] * 2 + [HBM] * 3 + [SMEM] * len(plan) + [ANY] * len(behind),
        out_specs=[HBM] * (2 * count) + [SMEM] * len(plan),
        out_shape=[out] * (2 * count - 1) + [longer if plan else out] + [table] * len(plan),
        scratch_shapes=scratch,
        compiler_params=params(63),
        cost_estimate=pl.CostEstimate(flops=3000000000, bytes_accessed=1, transcendentals=0),
        name="terms",
    )(sizes, mask, wave, left, right, *plan, *behind)


def add(a, b):
    return (a.astype(jnp.float32) + b.astype(jnp.float32)).astype(jnp.bfloat16)


def fetch_spill(rows, blocks, sent_ref, sources, target, sems):
    for j in range(SPILL):
        index = sent_ref[blocks * PIECES + j]
        for b in range(SPILL_BLOCKS):

            def copy(b=b, j=j, index=index):
                at = pl.ds(pl.multiple_of((index - b * PIECES) * rows, rows), rows)
                return pltpu.make_async_copy(sources[b].at[at], target.at[pl.ds(j * rows, rows)], sems.at[j])

            yield (index >= b * PIECES) & (index < (b + 1) * PIECES), copy


def run_copies(copies):
    copies = list(copies)
    for step in ("start", "wait"):
        for there, copy in copies:

            @pl.when(there)
            def _(copy=copy, step=step):
                getattr(copy(), step)()


def spill_kernel(rows, blocks, sent_ref, info_ref, *refs):
    own_refs, other_refs = refs[:SPILL_BLOCKS], refs[SPILL_BLOCKS : 2 * SPILL_BLOCKS]
    out_ref, own, other, mark, own_sems, other_sems = refs[2 * SPILL_BLOCKS + 1 :]
    flag = pltpu.make_async_copy(other_refs[-1].at[pl.ds(PIECES * rows, INFO)], mark, other_sems.at[SPILL])
    flag.start()
    run_copies(
        [*fetch_spill(rows, blocks, sent_ref, own_refs, own, own_sems), *fetch_spill(rows, blocks, sent_ref, other_refs, other, other_sems)]
    )
    out_ref[: SPILL * rows, :] = add(own[...], other[...])
    lane = lax.broadcasted_iota(jnp.int32, (INFO, TABLE), 1)
    flag.wait()
    more = jnp.maximum(mark[...].astype(jnp.float32).astype(jnp.int32), sent_ref[TABLE - 1])
    table = jnp.where(lane == TABLE - 1, more, info_ref[...])
    out_ref[SPILL * rows :, :] = table.astype(jnp.float32).astype(jnp.bfloat16)


def join_kernel(count, *refs):
    out_ref, held, come, go = refs[-4:]
    rows = refs[0].shape[0]
    arrive = [pltpu.make_async_copy(ref, held.at[pl.ds(i * rows, rows)], come.at[i]) for i, ref in enumerate(refs[:count])]
    for copy in arrive:
        copy.start()
    leave = []
    for i, copy in enumerate(arrive):
        copy.wait()
        at = pl.ds(i * rows, rows)
        leave.append(pltpu.make_async_copy(held.at[at], out_ref.at[at], go.at[i]))
        leave[-1].start()
    for copy in leave:
        copy.wait()


def join(behind, *parts):
    rows, width = parts[0].shape
    return pl.pallas_call(
        functools.partial(join_kernel, len(parts)),
        in_specs=[ANY] * (len(parts) + len(behind)),
        out_specs=HBM,
        out_shape=jax.ShapeDtypeStruct((len(parts) * rows, width), jnp.bfloat16),
        scratch_shapes=[pltpu.VMEM((len(parts) * rows, width), jnp.bfloat16)] + [pltpu.SemaphoreType.DMA((len(parts),))] * 2,
        compiler_params=params(63),
        name="join",
    )(*parts, *behind)


def pack_kernel(first, rows, pairs, sent_ref, *refs):
    own_refs, other_refs = refs[:pairs], refs[pairs : 2 * pairs]
    out_ref, stage, sems = refs[-3:]
    done = 0
    copies = []
    for own_ref, other_ref in zip(own_refs, other_refs):
        count = own_ref.shape[0] // rows
        stage[done * rows : (done + count) * rows, :] = add(own_ref[...], other_ref[: count * rows, :])
        for k in range(done, done + count):
            slot = sent_ref[first * PIECES + k]

            def copy(k=k, slot=slot):
                to = pl.ds(pl.multiple_of(slot * rows, rows), rows)
                return pltpu.make_async_copy(stage.at[pl.ds(k * rows, rows)], out_ref.at[to], sems.at[k])

            copies.append((slot >= 0, copy))

            @pl.when(slot >= 0)
            def _(copy=copy):
                copy().start()

        done += count
    for there, copy in copies:

        @pl.when(there)
        def _(copy=copy):
            copy().wait()


def pack(first, sent, own, other, packed, rows, slots, behind):
    total, width = sum(x.shape[0] for x in own), own[0].shape[1]
    before = [] if packed is None else [packed]
    pairs = len(own)
    return pl.pallas_call(
        functools.partial(pack_kernel, first, rows, pairs),
        in_specs=[SMEM] + [VMEM] * (2 * pairs) + [HBM] * len(before) + [ANY] * len(behind),
        out_specs=HBM,
        out_shape=jax.ShapeDtypeStruct((slots * rows, width), jnp.bfloat16),
        scratch_shapes=[pltpu.VMEM((total, width), jnp.bfloat16), pltpu.SemaphoreType.DMA((total // rows,))],
        input_output_aliases={1 + 2 * pairs: 0} if before else {},
        compiler_params=params(63),
        name="pack",
    )(sent, *own, *other, *before, *behind)


def list_kernel(rows, peers, blocks, *refs):
    sets, (order_ref, begin_ref, more_ref, lines, values, table, codes, count, sems) = refs[:4], refs[4:]
    me = lax.axis_index("sector")
    quarter = peers // 4
    chunk = SPILL * rows + INFO
    slots, targets = peers * SLOTS, blocks * PIECES
    copies = []
    for which, ref in enumerate(sets):
        for z in range(quarter):
            i = which * quarter + z
            copies.append(pltpu.make_async_copy(ref.at[pl.ds((z + 1) * chunk - INFO, INFO)], lines.at[i], sems.at[i]))
            copies[-1].start()
    for i in range(targets + 1):
        count[i] = 0
    for i, copy in enumerate(copies):
        copy.wait()
        values[i : i + 1, :] = lines[i].astype(jnp.float32).astype(jnp.int32)[:1, :]
    copy = pltpu.make_async_copy(values, table, sems.at[peers])
    copy.start()
    copy.wait()

    def note(i, code):
        to = jnp.where(code >= 0, code, targets)
        codes[i] = to
        count[to] += 1

    def source(j, more):
        apart = j ^ me
        line = ((apart & 1) * 2 + ((apart >> 1) & 1)) * quarter + (apart >> 2)
        for slot in range(SLOTS):
            note(j * SLOTS + slot, table[line, me * SLOTS + slot])
        for i in range(SPILL):
            owner = table[j, slots + i]
            note(slots + j * SPILL + i, jnp.where(owner == me, table[j, slots + SPILL + i], -1))
        return jnp.maximum(more, table[j, TABLE - 1])

    more_ref[0] = lax.fori_loop(0, peers, source, 0, unroll=4)

    def total(t, before):
        begin_ref[t] = before
        after = before + count[t]
        count[t] = before
        return after

    lax.fori_loop(0, targets + 1, total, 0, unroll=True)

    def put(i, _):
        code = codes[i]
        place = count[code]
        order_ref[place] = i
        count[code] = place + 1
        return 0

    lax.fori_loop(0, slots + peers * SPILL, put, 0, unroll=peers // 2)


def land_kernel(rows, peers, order_ref, begin_ref, arrived_ref, *refs):
    sets, (out_ref, held, stage, sems, out_sems) = refs[:4], refs[4:]
    quarter = peers // 4
    chunk = SPILL * rows + INFO
    slots = peers * SLOTS
    blocks, share, states = stage.shape
    width = states // COL_PARTS

    def at(start, unit=rows):
        return pl.ds(pl.multiple_of(start, unit), rows)

    def fetch(i, ref, start):
        return pltpu.make_async_copy(ref.at[at(start, 16)], held.at[at(i * rows)], sems.at[i])

    def begin(n, _):
        i = order_ref[n]

        @pl.when(i < slots)
        def _():
            fetch(i, arrived_ref, i * rows).start()

        @pl.when(i >= slots)
        def _():
            source, j = (i - slots) // SPILL, (i - slots) % SPILL
            for which in range(4):

                @pl.when(source // quarter == which)
                def _(which=which):
                    fetch(i, sets[which], source % quarter * chunk + j * rows).start()

        return 0

    lax.fori_loop(0, begin_ref[blocks * PIECES], begin, 0)

    copies = []
    for t in range(blocks):
        for k in range(PIECES):
            g, c = k // COL_PARTS, k % COL_PARTS
            first, last = begin_ref[t * PIECES + k], begin_ref[t * PIECES + k + 1]

            def more(n, total):
                i = order_ref[n]
                fetch(i, arrived_ref, 0).wait()
                return total + held[at(i * rows), :].astype(jnp.float32)

            total = lax.fori_loop(first, last, more, jnp.zeros((rows, width), jnp.float32))
            stage[t, g * rows : (g + 1) * rows, c * width : (c + 1) * width] = total.astype(jnp.bfloat16)
        copies.append(pltpu.make_async_copy(stage.at[t], out_ref.at[t], out_sems.at[t]))
        copies[-1].start()
    for copy in copies:
        copy.wait()


def two_halves(wavefunction, left_env, right_env, mpo_mask, block_size, route_owner, route_block):
    blocks, states, _ = wavefunction.shape
    share = states // 2
    rows = share // ROW_GROUPS
    width = states // COL_PARTS
    peers = lax.axis_size("sector")
    chunk = SPILL * rows + INFO

    def bf16(*shape):
        return jax.ShapeDtypeStruct(shape, jnp.bfloat16)

    def int32(*shape):
        return jax.ShapeDtypeStruct(shape, jnp.int32)

    def swap(x):
        return lax.ppermute(x, "mpo", [(0, 1), (1, 0)])

    def across(x, apart):
        return lax.ppermute(x, "sector", [(i, i ^ apart) for i in range(peers)])

    own, send, other = [], [], []

    def run(first, count, plan, behind):
        made = terms(first, count, block_size, mpo_mask, wavefunction, left_env[0], right_env[0], plan, behind)
        for n in range(count):
            own.append(made[2 * n])
            send.append(made[2 * n + 1])
            other.append(swap(send[-1]))
        return made[2 * count :]

    for b in range(SPILL_BLOCKS):
        tables = run(b, 1, [route_owner, route_block] if b == SPILL_BLOCKS - 1 else [], send[-1:])
    sent, info = tables
    run(SPILL_BLOCKS, blocks - SPILL_BLOCKS, [], send[-1:])

    spilled = pl.pallas_call(
        functools.partial(spill_kernel, rows, blocks),
        in_specs=[SMEM, VMEM] + [ANY] * (2 * SPILL_BLOCKS + 1),
        out_specs=VMEM,
        out_shape=bf16(chunk, width),
        scratch_shapes=[pltpu.VMEM((SPILL * rows, width), jnp.bfloat16)] * 2
        + [pltpu.VMEM((INFO, width), jnp.bfloat16)]
        + [pltpu.SemaphoreType.DMA((SPILL,)), pltpu.SemaphoreType.DMA((SPILL + 1,))],
        compiler_params=params(63),
        name="spill",
    )(sent, info.reshape(1, TABLE), *own[:SPILL_BLOCKS], *other[:SPILL_BLOCKS], send[-1])
    last = blocks - 1
    along = [across(spilled, apart) for apart in range(4, peers, 4)]
    packed = pack(0, sent, own[:last], other[:last], None, rows, peers * SLOTS, [])
    packed = pack(last, sent, own[last:], other[last:], packed, rows, peers * SLOTS, [])
    near = join([packed], spilled, *along)
    beside = across(near, 2)
    sets = [near, beside, across(near, 1), across(beside, 1)]
    arrived = lax.all_to_all(packed.reshape(peers, SLOTS * rows, width), "sector", split_axis=0, concat_axis=0, tiled=True)
    arrived = arrived.reshape(peers * SLOTS * rows, width)

    pieces = peers * (SLOTS + SPILL)
    order, begin, more = pl.pallas_call(
        functools.partial(list_kernel, rows, peers, blocks),
        in_specs=[ANY] * 4,
        out_specs=[SMEM] * 3,
        out_shape=[int32(pieces), int32(blocks * PIECES + 1), int32(1)],
        scratch_shapes=[
            pltpu.VMEM((peers, INFO, TABLE), jnp.bfloat16),
            pltpu.VMEM((peers, TABLE), jnp.int32),
            pltpu.SMEM((peers, TABLE), jnp.int32),
            pltpu.SMEM((pieces,), jnp.int32),
            pltpu.SMEM((blocks * PIECES + 1,), jnp.int32),
            pltpu.SemaphoreType.DMA((peers + 1,)),
        ],
        compiler_params=params(63),
        cost_estimate=pl.CostEstimate(flops=12000000000, bytes_accessed=0, transcendentals=0),
        name="list",
    )(*sets)

    def fast(order, begin, arrived, sets, *_):
        return pl.pallas_call(
            functools.partial(land_kernel, rows, peers),
            in_specs=[SMEM, SMEM] + [ANY] * 5,
            out_specs=HBM,
            out_shape=bf16(blocks, share, states),
            scratch_shapes=[
                pltpu.VMEM((pieces * rows, width), jnp.bfloat16),
                pltpu.VMEM((blocks, share, states), jnp.bfloat16),
                pltpu.SemaphoreType.DMA((pieces,)),
                pltpu.SemaphoreType.DMA((blocks,)),
            ],
            compiler_params=params(63),
            name="land",
        )(order, begin, arrived, *sets)

    def slow(order, begin, arrived, sets, own, other):
        sums = jnp.concatenate([add(a, b[: a.shape[0]]) for a, b in zip(own, other)], axis=0)
        sums = sums.reshape(blocks, ROW_GROUPS, COL_PARTS, rows, width).transpose(1, 3, 0, 2, 4)
        return exchange_all(sums.reshape(share, blocks, states), route_owner, route_block)

    return lax.cond(more[0] <= 0, fast, slow, order, begin, arrived, tuple(sets), tuple(own), tuple(other))


def solution(mesh):
    placed = (
        P("sector", None, None),
        P("mpo", "sector", None, None),
        P("mpo", "sector", None, None),
        P("mpo", "sector"),
        P("sector"),
        P("mpo", "sector", None),
        P("mpo", "sector", None),
    )

    def per_device(wavefunction, *rest):
        states = wavefunction.shape[1]
        peers = mesh.shape["sector"]
        fits = (
            mesh.shape["mpo"] == 2
            and peers >= 8
            and peers & (peers - 1) == 0
            and wavefunction.shape[0] == SLOTS + SPILL_BLOCKS
            and states // COL_PARTS == TABLE
            and states // (2 * ROW_GROUPS) % 16 == 0
            and peers * SLOTS + 2 * SPILL < TABLE
        )
        return (two_halves if fits else general)(wavefunction, *rest)

    return jax.shard_map(per_device, mesh=mesh, in_specs=placed, out_specs=P("sector", "mpo", None), check_vma=False)
```

```python
import functools

import jax
import jax.numpy as jnp
from jax import lax
from jax.experimental import pallas as pl
from jax.experimental.pallas import tpu as pltpu
from jax.sharding import PartitionSpec as P

ROW_GROUPS = 4
COL_PARTS = 2
PIECES = 8
SLOTS = 2
SPILL = 3
SPILL_BLOCKS = 2
CROSS = 8
INFO = 16
TABLE = 256

VMEM = pl.BlockSpec(memory_space=pltpu.VMEM)
SMEM = pl.BlockSpec(memory_space=pltpu.SMEM)
ANY = pl.BlockSpec(memory_space=pl.ANY)
HBM = pl.BlockSpec(memory_space=pltpu.HBM)


def params(mib):
    return pltpu.CompilerParams(vmem_limit_bytes=mib * 2**20)


def exchange_all(sigma_share, route_owner, route_block):
    row_count, block_count, states = sigma_share.shape
    group_rows = row_count // ROW_GROUPS
    width_part = states // COL_PARTS
    pieces = sigma_share.reshape(ROW_GROUPS, group_rows, block_count, COL_PARTS, width_part)
    pieces = pieces.transpose(2, 0, 3, 1, 4).reshape(block_count * PIECES, group_rows * width_part)
    owners = route_owner[0].reshape(-1)
    target_code = (route_block[0] * PIECES + jnp.arange(PIECES, dtype=jnp.int32)[None, :]).reshape(-1)
    peer_count = lax.axis_size("sector")
    capacity = min(block_count, max(2, (2 * block_count * PIECES + peer_count - 1) // peer_count))
    is_owner = (owners[:, None] == jnp.arange(peer_count, dtype=jnp.int32)[None, :]).astype(jnp.int32)
    before = jnp.cumsum(is_owner, axis=0) - is_owner
    position = jnp.sum(before * is_owner, axis=1)
    destination = owners * capacity + position
    slot_ids = jnp.arange(peer_count * capacity, dtype=jnp.int32)
    placing = slot_ids[:, None] == destination[None, :]
    send_data = jnp.dot(placing.astype(jnp.bfloat16), pieces, preferred_element_type=jnp.float32).astype(jnp.bfloat16)
    send_data = send_data.reshape(peer_count, capacity, group_rows * width_part)
    send_code = (jnp.sum(placing.astype(jnp.int32) * (target_code + 1)[None, :], axis=1) - 1).reshape(peer_count, capacity)
    arrived_data, arrived_code = (
        lax.all_to_all(send_data, "sector", split_axis=0, concat_axis=0, tiled=True),
        lax.all_to_all(send_code, "sector", split_axis=0, concat_axis=0, tiled=True),
    )
    arrived_data = arrived_data.reshape(peer_count * capacity, group_rows * width_part)
    arrived_code = arrived_code.reshape(-1)
    targets = jnp.arange(block_count * PIECES, dtype=jnp.int32)
    collect = (arrived_code[None, :] == targets[:, None]).astype(jnp.bfloat16)
    landed = jnp.dot(collect, arrived_data, preferred_element_type=jnp.float32).astype(jnp.bfloat16)
    landed = landed.reshape(block_count, ROW_GROUPS, COL_PARTS, group_rows, width_part)
    return landed.transpose(0, 1, 3, 2, 4).reshape(block_count, row_count, states)


def general(wavefunction, left_env, right_env, mpo_mask, block_size, route_owner, route_block):
    states = wavefunction.shape[1]
    row_count = states // lax.axis_size("mpo")
    positions = jnp.arange(states, dtype=jnp.int32)
    live_cols = positions[None, :] < block_size[:, None]
    live_mask = live_cols[:, :, None] & live_cols[:, None, :]
    masked = jnp.where(live_mask, wavefunction, jnp.zeros_like(wavefunction))
    right_part = jnp.einsum("bij,bkj->bik", masked, right_env[0], preferred_element_type=jnp.float32).astype(jnp.bfloat16)
    factor = mpo_mask[0].astype(jnp.float32)
    product = jnp.einsum("bij,bjk->ibk", left_env[0], right_part, preferred_element_type=jnp.float32)
    row_share = lax.psum_scatter(
        (product * factor[None, :, None]).astype(jnp.bfloat16), "mpo", scatter_dimension=0, tiled=True
    ).astype(jnp.float32)
    global_rows = lax.axis_index("mpo") * row_count + jnp.arange(row_count, dtype=jnp.int32)
    live_rows = global_rows[:, None] < block_size[None, :]
    share_mask = live_rows[:, :, None] & live_cols[None, :, :]
    sigma_share = jnp.where(share_mask, row_share, jnp.zeros_like(row_share)).astype(jnp.bfloat16)
    return exchange_all(sigma_share, route_owner, route_block)


def route(peers, blocks, group_rows, width, owner_ref, block_ref, size_ref, sent_ref, info_ref, count):
    first_row = lax.axis_index("mpo") * (ROW_GROUPS * group_rows)
    spill_at = peers * SLOTS
    for i in range(spill_at + 2 * SPILL):
        info_ref[i] = -1
    for i in range(SPILL):
        sent_ref[blocks * PIECES + i] = -1
    for i in range(peers):
        count[i] = 0

    nowhere = TABLE - 2

    def one(step, spilled):
        b, k = blocks - 1 - step // PIECES, step % PIECES
        i = b * PIECES + k
        g, c = k // COL_PARTS, k % COL_PARTS
        size = size_ref[b]
        live = (first_row + g * group_rows < size) & (c * width < size)
        owner = owner_ref[0, b, k]
        pos = count[owner]
        code = block_ref[0, b, k] * PIECES + k
        direct = live & (pos < SLOTS)
        kept = live & (pos >= SLOTS) & (spilled < SPILL)
        sent_ref[i] = jnp.where(direct, owner * SLOTS + pos, -1)
        info_ref[jnp.where(direct, owner * SLOTS + pos, nowhere)] = code
        count[owner] = pos + direct.astype(jnp.int32)
        sent_ref[jnp.where(kept, blocks * PIECES + spilled, nowhere)] = i
        info_ref[jnp.where(kept, spill_at + spilled, nowhere)] = owner
        info_ref[jnp.where(kept, spill_at + SPILL + spilled, nowhere)] = code
        return spilled + (live & (pos >= SLOTS)).astype(jnp.int32)

    spilled = lax.fori_loop(0, blocks * PIECES, one, 0, unroll=PIECES)
    sent_ref[TABLE - 1] = (spilled > SPILL).astype(jnp.int32)


def term_kernel(first, plan, size_ref, mask_ref, wave_ref, left_ref, right_ref, *refs):
    tables = ()
    if plan:
        tables = (*refs[:2], size_ref, *refs[-11:-9], refs[-1])
        refs = refs[2:-11] + refs[-9:-1]
    wave, left, right, own, send, mark, come, go = refs[-8:]
    results = refs[-8 - 2 * wave.shape[0] : -8]
    count, states, _ = wave.shape
    share = states // 2
    rows, width = share // ROW_GROUPS, states // COL_PARTS
    mine = lax.axis_index("mpo").astype(jnp.int32)
    arrive = []
    for n in range(count):
        arrive.append(
            [
                pltpu.make_async_copy(source.at[first + n], target.at[n], come.at[n, i])
                for i, (source, target) in enumerate(((wave_ref, wave), (right_ref, right), (left_ref, left)))
            ]
        )
        for copy in arrive[-1]:
            copy.start()
    leave = []
    if plan:
        route(*plan, *tables)
        mark[...] = jnp.full(mark.shape, tables[3][TABLE - 1], jnp.int32).astype(jnp.float32).astype(jnp.bfloat16)
        leave.append(pltpu.make_async_copy(mark, results[2 * count - 1].at[pl.ds(PIECES * rows, INFO)], go.at[count, 0]))
        leave[-1].start()
    row = lax.broadcasted_iota(jnp.int32, (states, states), 0)
    col = lax.broadcasted_iota(jnp.int32, (states, states), 1)
    for n in range(count):
        size = size_ref[first + n]
        active = mask_ref[0, first + n] != 0
        arrive[n][0].wait()
        masked = jnp.where((row < size) & (col < size), wave[n], jnp.zeros_like(wave[n]))
        arrive[n][1].wait()
        part = lax.dot_general(masked, right[n], (((1,), (1,)), ((), ())), preferred_element_type=jnp.float32)
        part = part.astype(jnp.bfloat16)
        arrive[n][2].wait()
        for which, (target, out_ref, half) in enumerate(((send, results[2 * n + 1], 1 - mine), (own, results[2 * n], mine))):
            start = pl.multiple_of(half * share, share)
            product = jnp.dot(left[n, pl.ds(start, share), :], part, preferred_element_type=jnp.float32)
            keep = (row[:share] + start < size) & (col[:share] < size) & active
            product = jnp.where(keep, product, 0.0).astype(jnp.bfloat16)
            for k in range(PIECES):
                g, c = k // COL_PARTS, k % COL_PARTS
                target[n, k * rows : (k + 1) * rows, :] = product[g * rows : (g + 1) * rows, c * width : (c + 1) * width]
            leave.append(pltpu.make_async_copy(target.at[n], out_ref.at[pl.ds(0, PIECES * rows)], go.at[n, which]))
            leave[-1].start()
    for copy in leave:
        copy.wait()


def terms(first, count, sizes, mask, wave, left, right, plan, behind):
    blocks, states, _ = wave.shape
    group_rows, width = states // 2 // ROW_GROUPS, states // COL_PARTS
    rows = PIECES * group_rows
    out = jax.ShapeDtypeStruct((rows, width), jnp.bfloat16)
    longer = jax.ShapeDtypeStruct((rows + INFO, width), jnp.bfloat16)
    table = jax.ShapeDtypeStruct((TABLE,), jnp.int32)
    peers = lax.axis_size("sector")
    scratch = [pltpu.VMEM((count, states, states), jnp.bfloat16)] * 3 + [pltpu.VMEM((count, rows, width), jnp.bfloat16)] * 2
    scratch += [pltpu.VMEM((INFO, width), jnp.bfloat16), pltpu.SemaphoreType.DMA((count, 3)), pltpu.SemaphoreType.DMA((count + 1, 2))]
    if plan:
        scratch += [pltpu.SMEM((peers,), jnp.int32)]
    return pl.pallas_call(
        functools.partial(term_kernel, first, (peers, blocks, group_rows, width) if plan else None),
        in_specs=[SMEM] * 2 + [HBM] * 3 + [SMEM] * len(plan) + [ANY] * len(behind),
        out_specs=[HBM] * (2 * count) + [SMEM] * len(plan),
        out_shape=[out] * (2 * count - 1) + [longer if plan else out] + [table] * len(plan),
        scratch_shapes=scratch,
        compiler_params=params(63),
        cost_estimate=pl.CostEstimate(flops=3000000000, bytes_accessed=1, transcendentals=0),
        name="terms",
    )(sizes, mask, wave, left, right, *plan, *behind)


def add(a, b):
    return (a.astype(jnp.float32) + b.astype(jnp.float32)).astype(jnp.bfloat16)


def fetch_spill(rows, blocks, sent_ref, sources, target, sems):
    for j in range(SPILL):
        index = sent_ref[blocks * PIECES + j]
        for b in range(SPILL_BLOCKS):

            def copy(b=b, j=j, index=index):
                at = pl.ds(pl.multiple_of((index - b * PIECES) * rows, rows), rows)
                return pltpu.make_async_copy(sources[b].at[at], target.at[pl.ds(j * rows, rows)], sems.at[j])

            yield (index >= b * PIECES) & (index < (b + 1) * PIECES), copy


def run_copies(copies):
    copies = list(copies)
    for step in ("start", "wait"):
        for there, copy in copies:

            @pl.when(there)
            def _(copy=copy, step=step):
                getattr(copy(), step)()


def spill_kernel(rows, blocks, sent_ref, info_ref, *refs):
    own_refs, other_refs = refs[:SPILL_BLOCKS], refs[SPILL_BLOCKS : 2 * SPILL_BLOCKS]
    out_ref, own, other, mark, own_sems, other_sems = refs[2 * SPILL_BLOCKS + 1 :]
    flag = pltpu.make_async_copy(other_refs[-1].at[pl.ds(PIECES * rows, INFO)], mark, other_sems.at[SPILL])
    flag.start()
    run_copies(
        [*fetch_spill(rows, blocks, sent_ref, own_refs, own, own_sems), *fetch_spill(rows, blocks, sent_ref, other_refs, other, other_sems)]
    )
    out_ref[: SPILL * rows, :] = add(own[...], other[...])
    lane = lax.broadcasted_iota(jnp.int32, (INFO, TABLE), 1)
    flag.wait()
    more = jnp.maximum(mark[...].astype(jnp.float32).astype(jnp.int32), sent_ref[TABLE - 1])
    table = jnp.where(lane == TABLE - 1, more, info_ref[...])
    out_ref[SPILL * rows :, :] = table.astype(jnp.float32).astype(jnp.bfloat16)


def join_kernel(rows, peers, count, *refs):
    near_ref, tables_ref, cross_ref, held, values, table, come, go = refs[-8:]
    me = lax.axis_index("sector").astype(jnp.int32)
    chunk = refs[0].shape[0]
    spill_at = peers * SLOTS
    arrive = [pltpu.make_async_copy(ref, held.at[pl.ds(i * chunk, chunk)], come.at[i]) for i, ref in enumerate(refs[:count])]
    for copy in arrive:
        copy.start()
    leave = []
    for i, copy in enumerate(arrive):
        copy.wait()
        at, info = pl.ds(i * chunk, chunk), pl.ds((i + 1) * chunk - INFO, INFO)
        leave.append(pltpu.make_async_copy(held.at[info], tables_ref.at[pl.ds(i * INFO, INFO)], go.at[count + i]))
        leave.append(pltpu.make_async_copy(held.at[at], near_ref.at[at], go.at[i]))
        leave[-2].start()
        leave[-1].start()
        values[i : i + 1, :] = held[(i + 1) * chunk - INFO : (i + 1) * chunk, :].astype(jnp.float32).astype(jnp.int32)[:1, :]
    copy = pltpu.make_async_copy(values, table, go.at[2 * count])
    copy.start()
    copy.wait()
    moves = []
    place = 0
    for i in range(count):
        for j in range(SPILL):
            owner = table[i, spill_at + j]
            there = (owner >= 0) & (owner // 4 == me // 4) & ((owner ^ me) & 2 == 2)
            fits = there & (place < CROSS)

            def move(i=i, j=j, place=place):
                to = pl.ds(pl.multiple_of(place * rows, rows), rows)
                sem = go.at[2 * count + 1 + i * SPILL + j]
                return pltpu.make_async_copy(held.at[pl.ds(i * chunk + j * rows, rows)], cross_ref.at[to], sem)

            moves.append((fits, move))
            place = place + there.astype(jnp.int32)
    run_copies(moves)
    for copy in leave:
        copy.wait()


def join(rows, peers, behind, *parts):
    chunk, width = parts[0].shape
    count = len(parts)
    return pl.pallas_call(
        functools.partial(join_kernel, rows, peers, count),
        in_specs=[ANY] * (count + len(behind)),
        out_specs=[HBM] * 3,
        out_shape=[jax.ShapeDtypeStruct((n, width), jnp.bfloat16) for n in (count * chunk, count * INFO, CROSS * rows)],
        scratch_shapes=[
            pltpu.VMEM((count * chunk, width), jnp.bfloat16),
            pltpu.VMEM((count, TABLE), jnp.int32),
            pltpu.SMEM((count, TABLE), jnp.int32),
            pltpu.SemaphoreType.DMA((count,)),
            pltpu.SemaphoreType.DMA((2 * count + 1 + count * SPILL,)),
        ],
        compiler_params=params(63),
        name="join",
    )(*parts, *behind)


def pack_kernel(first, rows, pairs, sent_ref, *refs):
    own_refs, other_refs = refs[:pairs], refs[pairs : 2 * pairs]
    out_ref, stage, sems = refs[-3:]
    done = 0
    copies = []
    for own_ref, other_ref in zip(own_refs, other_refs):
        count = own_ref.shape[0] // rows
        stage[done * rows : (done + count) * rows, :] = add(own_ref[...], other_ref[: count * rows, :])
        for k in range(done, done + count):
            slot = sent_ref[first * PIECES + k]

            def copy(k=k, slot=slot):
                to = pl.ds(pl.multiple_of(slot * rows, rows), rows)
                return pltpu.make_async_copy(stage.at[pl.ds(k * rows, rows)], out_ref.at[to], sems.at[k])

            copies.append((slot >= 0, copy))

            @pl.when(slot >= 0)
            def _(copy=copy):
                copy().start()

        done += count
    for there, copy in copies:

        @pl.when(there)
        def _(copy=copy):
            copy().wait()


def pack(first, sent, own, other, packed, rows, slots, behind):
    total, width = sum(x.shape[0] for x in own), own[0].shape[1]
    before = [] if packed is None else [packed]
    pairs = len(own)
    return pl.pallas_call(
        functools.partial(pack_kernel, first, rows, pairs),
        in_specs=[SMEM] + [VMEM] * (2 * pairs) + [HBM] * len(before) + [ANY] * len(behind),
        out_specs=HBM,
        out_shape=jax.ShapeDtypeStruct((slots * rows, width), jnp.bfloat16),
        scratch_shapes=[pltpu.VMEM((total, width), jnp.bfloat16), pltpu.SemaphoreType.DMA((total // rows,))],
        input_output_aliases={1 + 2 * pairs: 0} if before else {},
        compiler_params=params(63),
        name="pack",
    )(sent, *own, *other, *before, *behind)


def list_kernel(rows, peers, blocks, *refs):
    sets, (order_ref, begin_ref, where_ref, more_ref, lines, values, table, codes, count, cross, sems) = refs[:4], refs[4:]
    me = lax.axis_index("sector")
    quarter = peers // 4
    chunk = SPILL * rows + INFO
    slots, targets = peers * SLOTS, blocks * PIECES
    copies = []
    for which, ref in enumerate(sets):
        for z in range(quarter):
            i = which * quarter + z
            copies.append(pltpu.make_async_copy(ref.at[pl.ds(z * INFO, INFO)], lines.at[i], sems.at[i]))
            copies[-1].start()
    for i in range(targets + 1):
        count[i] = 0
    for i, copy in enumerate(copies):
        copy.wait()
        values[i : i + 1, :] = lines[i].astype(jnp.float32).astype(jnp.int32)[:1, :]
    copy = pltpu.make_async_copy(values, table, sems.at[peers])
    copy.start()
    copy.wait()

    def note(i, code):
        to = jnp.where(code >= 0, code, targets)
        codes[i] = to
        count[to] += 1

    def source(j, more):
        apart = j ^ me
        line = ((apart & 1) * 2 + ((apart >> 1) & 1)) * quarter + (apart >> 2)
        for slot in range(SLOTS):
            note(j * SLOTS + slot, table[line, me * SLOTS + slot])
        for i in range(SPILL):
            owner = table[j, slots + i]
            note(slots + j * SPILL + i, jnp.where(owner == me, table[j, slots + SPILL + i], -1))
        return jnp.maximum(more, table[j, TABLE - 1])

    more = lax.fori_loop(0, peers, source, 0, unroll=4)

    for i in range(peers):
        cross[i] = 0

    def passed(line, place):
        which, z = line // quarter, line % quarter
        origin = me ^ (z * 4 + which % 2 * 2 + which // 2)
        place = jnp.where(z == 0, 0, place)
        for j in range(SPILL):
            owner = table[line, slots + j]
            change = (owner >= 0) & ((owner ^ origin) & 2 == 2)
            to = jnp.maximum(owner, 0) // 4 * 4 + origin % 4
            cross[to] += change.astype(jnp.int32)
            where_ref[line * SPILL + j] = place
            place = place + (change & (owner // 4 == me // 4)).astype(jnp.int32)
        return place

    lax.fori_loop(0, peers, passed, 0, unroll=4)
    for i in range(peers):
        more = jnp.maximum(more, (cross[i] > CROSS).astype(jnp.int32))
    more_ref[0] = more

    def total(t, before):
        begin_ref[t] = before
        after = before + count[t]
        count[t] = before
        return after

    lax.fori_loop(0, targets + 1, total, 0, unroll=True)

    def put(i, _):
        code = codes[i]
        place = count[code]
        order_ref[place] = i
        count[code] = place + 1
        return 0

    lax.fori_loop(0, slots + peers * SPILL, put, 0, unroll=peers // 2)


def land_kernel(rows, peers, order_ref, begin_ref, where_ref, arrived_ref, *refs):
    sets, (out_ref, held, stage, sems, out_sems) = refs[:4], refs[4:]
    quarter = peers // 4
    chunk = SPILL * rows + INFO
    slots = peers * SLOTS
    blocks, share, states = stage.shape
    width = states // COL_PARTS

    def at(start, unit=rows):
        return pl.ds(pl.multiple_of(start, unit), rows)

    def fetch(i, ref, start):
        return pltpu.make_async_copy(ref.at[at(start, 16)], held.at[at(i * rows)], sems.at[i])

    def begin(n, _):
        i = order_ref[n]

        @pl.when(i < slots)
        def _():
            fetch(i, arrived_ref, i * rows).start()

        @pl.when(i >= slots)
        def _():
            source, j = (i - slots) // SPILL, (i - slots) % SPILL
            for which in range(4):

                @pl.when(source // quarter == which)
                def _(which=which):
                    start = where_ref[i - slots] * rows if which % 2 else source % quarter * chunk + j * rows
                    fetch(i, sets[which], start).start()

        return 0

    lax.fori_loop(0, begin_ref[blocks * PIECES], begin, 0)

    copies = []
    for t in range(blocks):
        for k in range(PIECES):
            g, c = k // COL_PARTS, k % COL_PARTS
            first, last = begin_ref[t * PIECES + k], begin_ref[t * PIECES + k + 1]

            def more(n, total):
                i = order_ref[n]
                fetch(i, arrived_ref, 0).wait()
                return total + held[at(i * rows), :].astype(jnp.float32)

            total = lax.fori_loop(first, last, more, jnp.zeros((rows, width), jnp.float32))
            stage[t, g * rows : (g + 1) * rows, c * width : (c + 1) * width] = total.astype(jnp.bfloat16)
        copies.append(pltpu.make_async_copy(stage.at[t], out_ref.at[t], out_sems.at[t]))
        copies[-1].start()
    for copy in copies:
        copy.wait()


def two_halves(wavefunction, left_env, right_env, mpo_mask, block_size, route_owner, route_block):
    blocks, states, _ = wavefunction.shape
    share = states // 2
    rows = share // ROW_GROUPS
    width = states // COL_PARTS
    peers = lax.axis_size("sector")
    chunk = SPILL * rows + INFO

    def bf16(*shape):
        return jax.ShapeDtypeStruct(shape, jnp.bfloat16)

    def int32(*shape):
        return jax.ShapeDtypeStruct(shape, jnp.int32)

    def swap(x):
        return lax.ppermute(x, "mpo", [(0, 1), (1, 0)])

    def across(x, apart):
        return lax.ppermute(x, "sector", [(i, i ^ apart) for i in range(peers)])

    own, send, other = [], [], []

    def run(first, count, plan, behind):
        made = terms(first, count, block_size, mpo_mask, wavefunction, left_env[0], right_env[0], plan, behind)
        for n in range(count):
            own.append(made[2 * n])
            send.append(made[2 * n + 1])
            other.append(swap(send[-1]))
        return made[2 * count :]

    for b in range(SPILL_BLOCKS):
        tables = run(b, 1, [route_owner, route_block] if b == SPILL_BLOCKS - 1 else [], send[-1:])
    sent, info = tables
    run(SPILL_BLOCKS, blocks - SPILL_BLOCKS, [], send[-1:])

    spilled = pl.pallas_call(
        functools.partial(spill_kernel, rows, blocks),
        in_specs=[SMEM, VMEM] + [HBM] * (2 * SPILL_BLOCKS) + [ANY],
        out_specs=VMEM,
        out_shape=bf16(chunk, width),
        scratch_shapes=[pltpu.VMEM((SPILL * rows, width), jnp.bfloat16)] * 2
        + [pltpu.VMEM((INFO, width), jnp.bfloat16)]
        + [pltpu.SemaphoreType.DMA((SPILL,)), pltpu.SemaphoreType.DMA((SPILL + 1,))],
        compiler_params=params(63),
        name="spill",
    )(sent, info.reshape(1, TABLE), *own[:SPILL_BLOCKS], *other[:SPILL_BLOCKS], send[-1])
    last = blocks - 1
    along = [across(spilled, apart) for apart in range(4, peers, 4)]
    packed = pack(0, sent, own[:last], other[:last], None, rows, peers * SLOTS, [])
    packed = pack(last, sent, own[last:], other[last:], packed, rows, peers * SLOTS, [])
    near, tables, crossing = join(rows, peers, [packed], spilled, *along)
    tables_beside, tables_mate = across(tables, 2), across(tables, 1)
    tables = [tables, tables_beside, tables_mate, across(tables_beside, 1)]
    beside = across(crossing, 2)
    arrived = lax.all_to_all(packed.reshape(peers, SLOTS * rows, width), "sector", split_axis=0, concat_axis=0, tiled=True)
    arrived = arrived.reshape(peers * SLOTS * rows, width)

    pieces = peers * (SLOTS + SPILL)
    order, begin, where, more = pl.pallas_call(
        functools.partial(list_kernel, rows, peers, blocks),
        in_specs=[HBM] * 4,
        out_specs=[SMEM] * 4,
        out_shape=[int32(pieces), int32(blocks * PIECES + 1), int32(peers * SPILL), int32(1)],
        scratch_shapes=[
            pltpu.VMEM((peers, INFO, TABLE), jnp.bfloat16),
            pltpu.VMEM((peers, TABLE), jnp.int32),
            pltpu.SMEM((peers, TABLE), jnp.int32),
            pltpu.SMEM((pieces,), jnp.int32),
            pltpu.SMEM((blocks * PIECES + 1,), jnp.int32),
            pltpu.SMEM((peers,), jnp.int32),
            pltpu.SemaphoreType.DMA((peers + 1,)),
        ],
        compiler_params=params(63),
        cost_estimate=pl.CostEstimate(flops=17000000000, bytes_accessed=0, transcendentals=0),
        name="list",
    )(*tables)

    more = jnp.maximum(more, swap(more))
    beside, begin, more = lax.optimization_barrier((beside, begin, more))
    sets = [near, beside, across(near, 1), across(beside, 1)]

    def fast(order, begin, where, arrived, sets, *_):
        return pl.pallas_call(
            functools.partial(land_kernel, rows, peers),
            in_specs=[SMEM] * 3 + [ANY] * 5,
            out_specs=HBM,
            out_shape=bf16(blocks, share, states),
            scratch_shapes=[
                pltpu.VMEM((pieces * rows, width), jnp.bfloat16),
                pltpu.VMEM((blocks, share, states), jnp.bfloat16),
                pltpu.SemaphoreType.DMA((pieces,)),
                pltpu.SemaphoreType.DMA((blocks,)),
            ],
            compiler_params=params(63),
            name="land",
        )(order, begin, where, arrived, *sets)

    def slow(order, begin, where, arrived, sets, own, other):
        sums = jnp.concatenate([add(a, b[: a.shape[0]]) for a, b in zip(own, other)], axis=0)
        sums = sums.reshape(blocks, ROW_GROUPS, COL_PARTS, rows, width).transpose(1, 3, 0, 2, 4)
        return exchange_all(sums.reshape(share, blocks, states), route_owner, route_block)

    return lax.cond(more[0] <= 0, fast, slow, order, begin, where, arrived, tuple(sets), tuple(own), tuple(other))


def solution(mesh):
    placed = (
        P("sector", None, None),
        P("mpo", "sector", None, None),
        P("mpo", "sector", None, None),
        P("mpo", "sector"),
        P("sector"),
        P("mpo", "sector", None),
        P("mpo", "sector", None),
    )

    def per_device(wavefunction, *rest):
        states = wavefunction.shape[1]
        peers = mesh.shape["sector"]
        fits = (
            mesh.shape["mpo"] == 2
            and peers >= 8
            and peers & (peers - 1) == 0
            and wavefunction.shape[0] == SLOTS + SPILL_BLOCKS
            and states // COL_PARTS == TABLE
            and states // (2 * ROW_GROUPS) % 16 == 0
            and peers * SLOTS + 2 * SPILL < TABLE
        )
        return (two_halves if fits else general)(wavefunction, *rest)

    return jax.shard_map(per_device, mesh=mesh, in_specs=placed, out_specs=P("sector", "mpo", None), check_vma=False)
```

```python
import functools

import jax
import jax.numpy as jnp
from jax import lax
from jax.experimental import pallas as pl
from jax.experimental.pallas import tpu as pltpu
from jax.sharding import PartitionSpec as P

ROW_GROUPS = 4
COL_PARTS = 2
PIECES = 8
SLOTS = 2
SPILL = 3
SPILL_BLOCKS = 2
CROSS = 8
INFO = 16
TABLE = 256

VMEM = pl.BlockSpec(memory_space=pltpu.VMEM)
SMEM = pl.BlockSpec(memory_space=pltpu.SMEM)
ANY = pl.BlockSpec(memory_space=pl.ANY)
HBM = pl.BlockSpec(memory_space=pltpu.HBM)


def params(mib):
    return pltpu.CompilerParams(vmem_limit_bytes=mib * 2**20)


def exchange_all(sigma_share, route_owner, route_block):
    row_count, block_count, states = sigma_share.shape
    group_rows = row_count // ROW_GROUPS
    width_part = states // COL_PARTS
    pieces = sigma_share.reshape(ROW_GROUPS, group_rows, block_count, COL_PARTS, width_part)
    pieces = pieces.transpose(2, 0, 3, 1, 4).reshape(block_count * PIECES, group_rows * width_part)
    owners = route_owner[0].reshape(-1)
    target_code = (route_block[0] * PIECES + jnp.arange(PIECES, dtype=jnp.int32)[None, :]).reshape(-1)
    peer_count = lax.axis_size("sector")
    capacity = min(block_count, max(2, (2 * block_count * PIECES + peer_count - 1) // peer_count))
    is_owner = (owners[:, None] == jnp.arange(peer_count, dtype=jnp.int32)[None, :]).astype(jnp.int32)
    before = jnp.cumsum(is_owner, axis=0) - is_owner
    position = jnp.sum(before * is_owner, axis=1)
    destination = owners * capacity + position
    slot_ids = jnp.arange(peer_count * capacity, dtype=jnp.int32)
    placing = slot_ids[:, None] == destination[None, :]
    send_data = jnp.dot(placing.astype(jnp.bfloat16), pieces, preferred_element_type=jnp.float32).astype(jnp.bfloat16)
    send_data = send_data.reshape(peer_count, capacity, group_rows * width_part)
    send_code = (jnp.sum(placing.astype(jnp.int32) * (target_code + 1)[None, :], axis=1) - 1).reshape(peer_count, capacity)
    arrived_data, arrived_code = (
        lax.all_to_all(send_data, "sector", split_axis=0, concat_axis=0, tiled=True),
        lax.all_to_all(send_code, "sector", split_axis=0, concat_axis=0, tiled=True),
    )
    arrived_data = arrived_data.reshape(peer_count * capacity, group_rows * width_part)
    arrived_code = arrived_code.reshape(-1)
    targets = jnp.arange(block_count * PIECES, dtype=jnp.int32)
    collect = (arrived_code[None, :] == targets[:, None]).astype(jnp.bfloat16)
    landed = jnp.dot(collect, arrived_data, preferred_element_type=jnp.float32).astype(jnp.bfloat16)
    landed = landed.reshape(block_count, ROW_GROUPS, COL_PARTS, group_rows, width_part)
    return landed.transpose(0, 1, 3, 2, 4).reshape(block_count, row_count, states)


def general(wavefunction, left_env, right_env, mpo_mask, block_size, route_owner, route_block):
    states = wavefunction.shape[1]
    row_count = states // lax.axis_size("mpo")
    positions = jnp.arange(states, dtype=jnp.int32)
    live_cols = positions[None, :] < block_size[:, None]
    live_mask = live_cols[:, :, None] & live_cols[:, None, :]
    masked = jnp.where(live_mask, wavefunction, jnp.zeros_like(wavefunction))
    right_part = jnp.einsum("bij,bkj->bik", masked, right_env[0], preferred_element_type=jnp.float32).astype(jnp.bfloat16)
    factor = mpo_mask[0].astype(jnp.float32)
    product = jnp.einsum("bij,bjk->ibk", left_env[0], right_part, preferred_element_type=jnp.float32)
    row_share = lax.psum_scatter(
        (product * factor[None, :, None]).astype(jnp.bfloat16), "mpo", scatter_dimension=0, tiled=True
    ).astype(jnp.float32)
    global_rows = lax.axis_index("mpo") * row_count + jnp.arange(row_count, dtype=jnp.int32)
    live_rows = global_rows[:, None] < block_size[None, :]
    share_mask = live_rows[:, :, None] & live_cols[None, :, :]
    sigma_share = jnp.where(share_mask, row_share, jnp.zeros_like(row_share)).astype(jnp.bfloat16)
    return exchange_all(sigma_share, route_owner, route_block)


def route(peers, blocks, group_rows, width, owner_ref, block_ref, size_ref, sent_ref, info_ref, count):
    first_row = lax.axis_index("mpo") * (ROW_GROUPS * group_rows)
    spill_at = peers * SLOTS
    for i in range(spill_at + 2 * SPILL):
        info_ref[i] = -1
    for i in range(SPILL):
        sent_ref[blocks * PIECES + i] = -1
    for i in range(peers):
        count[i] = 0

    nowhere = TABLE - 2

    def one(step, spilled):
        b, k = blocks - 1 - step // PIECES, step % PIECES
        i = b * PIECES + k
        g, c = k // COL_PARTS, k % COL_PARTS
        size = size_ref[b]
        live = (first_row + g * group_rows < size) & (c * width < size)
        owner = owner_ref[0, b, k]
        pos = count[owner]
        code = block_ref[0, b, k] * PIECES + k
        direct = live & (pos < SLOTS)
        kept = live & (pos >= SLOTS) & (spilled < SPILL)
        sent_ref[i] = jnp.where(direct, owner * SLOTS + pos, -1)
        info_ref[jnp.where(direct, owner * SLOTS + pos, nowhere)] = code
        count[owner] = pos + direct.astype(jnp.int32)
        sent_ref[jnp.where(kept, blocks * PIECES + spilled, nowhere)] = i
        info_ref[jnp.where(kept, spill_at + spilled, nowhere)] = owner
        info_ref[jnp.where(kept, spill_at + SPILL + spilled, nowhere)] = code
        return spilled + (live & (pos >= SLOTS)).astype(jnp.int32)

    spilled = lax.fori_loop(0, blocks * PIECES, one, 0, unroll=PIECES)
    sent_ref[TABLE - 1] = (spilled > SPILL).astype(jnp.int32)


def term_kernel(first, plan, size_ref, mask_ref, wave_ref, left_ref, right_ref, *refs):
    tables = ()
    if plan:
        tables = (*refs[:2], size_ref, *refs[-10:-8], refs[-1])
        refs = refs[2:-10] + refs[-8:-1]
    wave, left, right, own, send, come, go = refs[-7:]
    results = refs[-7 - 2 * wave.shape[0] : -7]
    count, states, _ = wave.shape
    share = states // 2
    rows, width = share // ROW_GROUPS, states // COL_PARTS
    mine = lax.axis_index("mpo").astype(jnp.int32)
    arrive = []
    for n in range(count):
        arrive.append(
            [
                pltpu.make_async_copy(source.at[first + n], target.at[n], come.at[n, i])
                for i, (source, target) in enumerate(((wave_ref, wave), (right_ref, right), (left_ref, left)))
            ]
        )
        for copy in arrive[-1]:
            copy.start()
    leave = []
    if plan:
        route(*plan, *tables)
    row = lax.broadcasted_iota(jnp.int32, (states, states), 0)
    col = lax.broadcasted_iota(jnp.int32, (states, states), 1)
    for n in range(count):
        size = size_ref[first + n]
        active = mask_ref[0, first + n] != 0
        arrive[n][0].wait()
        masked = jnp.where((row < size) & (col < size), wave[n], jnp.zeros_like(wave[n]))
        arrive[n][1].wait()
        part = lax.dot_general(masked, right[n], (((1,), (1,)), ((), ())), preferred_element_type=jnp.float32)
        part = part.astype(jnp.bfloat16)
        arrive[n][2].wait()
        for which, (target, out_ref, half) in enumerate(((send, results[2 * n + 1], 1 - mine), (own, results[2 * n], mine))):
            start = pl.multiple_of(half * share, share)
            product = jnp.dot(left[n, pl.ds(start, share), :], part, preferred_element_type=jnp.float32)
            keep = (row[:share] + start < size) & (col[:share] < size) & active
            product = jnp.where(keep, product, 0.0).astype(jnp.bfloat16)
            for k in range(PIECES):
                g, c = k // COL_PARTS, k % COL_PARTS
                target[n, k * rows : (k + 1) * rows, :] = product[g * rows : (g + 1) * rows, c * width : (c + 1) * width]
            leave.append(pltpu.make_async_copy(target.at[n], out_ref, go.at[n, which]))
            leave[-1].start()
    for copy in leave:
        copy.wait()


def terms(first, count, sizes, mask, wave, left, right, plan, behind):
    blocks, states, _ = wave.shape
    group_rows, width = states // 2 // ROW_GROUPS, states // COL_PARTS
    rows = PIECES * group_rows
    out = jax.ShapeDtypeStruct((rows, width), jnp.bfloat16)
    table = jax.ShapeDtypeStruct((TABLE,), jnp.int32)
    peers = lax.axis_size("sector")
    scratch = [pltpu.VMEM((count, states, states), jnp.bfloat16)] * 3 + [pltpu.VMEM((count, rows, width), jnp.bfloat16)] * 2
    scratch += [pltpu.SemaphoreType.DMA((count, 3)), pltpu.SemaphoreType.DMA((count, 2))]
    if plan:
        scratch += [pltpu.SMEM((peers,), jnp.int32)]
    return pl.pallas_call(
        functools.partial(term_kernel, first, (peers, blocks, group_rows, width) if plan else None),
        in_specs=[SMEM] * 2 + [HBM] * 3 + [SMEM] * len(plan) + [ANY] * len(behind),
        out_specs=[HBM] * (2 * count) + [SMEM] * len(plan),
        out_shape=[out] * (2 * count) + [table] * len(plan),
        scratch_shapes=scratch,
        compiler_params=params(63),
        cost_estimate=pl.CostEstimate(flops=3000000000, bytes_accessed=1, transcendentals=0),
        name="terms",
    )(sizes, mask, wave, left, right, *plan, *behind)


def add(a, b):
    return (a.astype(jnp.float32) + b.astype(jnp.float32)).astype(jnp.bfloat16)


def fetch_spill(rows, blocks, sent_ref, sources, target, sems):
    for j in range(SPILL):
        index = sent_ref[blocks * PIECES + j]
        for b in range(SPILL_BLOCKS):

            def copy(b=b, j=j, index=index):
                at = pl.ds(pl.multiple_of((index - b * PIECES) * rows, rows), rows)
                return pltpu.make_async_copy(sources[b].at[at], target.at[pl.ds(j * rows, rows)], sems.at[j])

            yield (index >= b * PIECES) & (index < (b + 1) * PIECES), copy


def run_copies(copies):
    copies = list(copies)
    for step in ("start", "wait"):
        for there, copy in copies:

            @pl.when(there)
            def _(copy=copy, step=step):
                getattr(copy(), step)()


def spill_kernel(rows, blocks, sent_ref, info_ref, *refs):
    own_refs, other_refs = refs[:SPILL_BLOCKS], refs[SPILL_BLOCKS : 2 * SPILL_BLOCKS]
    out_ref, own, other, own_sems, other_sems = refs[2 * SPILL_BLOCKS + 1 :]
    run_copies(
        [*fetch_spill(rows, blocks, sent_ref, own_refs, own, own_sems), *fetch_spill(rows, blocks, sent_ref, other_refs, other, other_sems)]
    )
    out_ref[: SPILL * rows, :] = add(own[...], other[...])
    lane = lax.broadcasted_iota(jnp.int32, (INFO, TABLE), 1)
    table = jnp.where(lane == TABLE - 1, sent_ref[TABLE - 1], info_ref[...])
    out_ref[SPILL * rows :, :] = table.astype(jnp.float32).astype(jnp.bfloat16)


def join_kernel(rows, peers, count, *refs):
    near_ref, tables_ref, cross_ref, held, values, table, come, go = refs[-8:]
    me = lax.axis_index("sector").astype(jnp.int32)
    chunk = refs[0].shape[0]
    spill_at = peers * SLOTS
    arrive = [pltpu.make_async_copy(ref, held.at[pl.ds(i * chunk, chunk)], come.at[i]) for i, ref in enumerate(refs[:count])]
    for copy in arrive:
        copy.start()
    leave = []
    for i, copy in enumerate(arrive):
        copy.wait()
        at, info = pl.ds(i * chunk, chunk), pl.ds((i + 1) * chunk - INFO, INFO)
        leave.append(pltpu.make_async_copy(held.at[info], tables_ref.at[pl.ds(i * INFO, INFO)], go.at[count + i]))
        leave.append(pltpu.make_async_copy(held.at[at], near_ref.at[at], go.at[i]))
        leave[-2].start()
        leave[-1].start()
        values[i : i + 1, :] = held[(i + 1) * chunk - INFO : (i + 1) * chunk, :].astype(jnp.float32).astype(jnp.int32)[:1, :]
    copy = pltpu.make_async_copy(values, table, go.at[2 * count])
    copy.start()
    copy.wait()
    moves = []
    place = 0
    for i in range(count):
        for j in range(SPILL):
            owner = table[i, spill_at + j]
            there = (owner >= 0) & (owner // 4 == me // 4) & ((owner ^ me) & 2 == 2)
            fits = there & (place < CROSS)

            def move(i=i, j=j, place=place):
                to = pl.ds(pl.multiple_of(place * rows, rows), rows)
                sem = go.at[2 * count + 1 + i * SPILL + j]
                return pltpu.make_async_copy(held.at[pl.ds(i * chunk + j * rows, rows)], cross_ref.at[to], sem)

            moves.append((fits, move))
            place = place + there.astype(jnp.int32)
    run_copies(moves)
    for copy in leave:
        copy.wait()


def join(rows, peers, behind, *parts):
    chunk, width = parts[0].shape
    count = len(parts)
    return pl.pallas_call(
        functools.partial(join_kernel, rows, peers, count),
        in_specs=[ANY] * (count + len(behind)),
        out_specs=[HBM] * 3,
        out_shape=[jax.ShapeDtypeStruct((n, width), jnp.bfloat16) for n in (count * chunk, count * INFO, CROSS * rows)],
        scratch_shapes=[
            pltpu.VMEM((count * chunk, width), jnp.bfloat16),
            pltpu.VMEM((count, TABLE), jnp.int32),
            pltpu.SMEM((count, TABLE), jnp.int32),
            pltpu.SemaphoreType.DMA((count,)),
            pltpu.SemaphoreType.DMA((2 * count + 1 + count * SPILL,)),
        ],
        compiler_params=params(16),
        name="join",
    )(*parts, *behind)


def pack_kernel(first, rows, pairs, sent_ref, *refs):
    own_refs, other_refs = refs[:pairs], refs[pairs : 2 * pairs]
    out_ref, stage, sems = refs[-3:]
    done = 0
    copies = []
    for own_ref, other_ref in zip(own_refs, other_refs):
        count = own_ref.shape[0] // rows
        stage[done * rows : (done + count) * rows, :] = add(own_ref[...], other_ref[: count * rows, :])
        for k in range(done, done + count):
            slot = sent_ref[first * PIECES + k]

            def copy(k=k, slot=slot):
                to = pl.ds(pl.multiple_of(slot * rows, rows), rows)
                return pltpu.make_async_copy(stage.at[pl.ds(k * rows, rows)], out_ref.at[to], sems.at[k])

            copies.append((slot >= 0, copy))

            @pl.when(slot >= 0)
            def _(copy=copy):
                copy().start()

        done += count
    for there, copy in copies:

        @pl.when(there)
        def _(copy=copy):
            copy().wait()


def pack(first, sent, own, other, packed, rows, slots, behind):
    total, width = sum(x.shape[0] for x in own), own[0].shape[1]
    before = [] if packed is None else [packed]
    pairs = len(own)
    return pl.pallas_call(
        functools.partial(pack_kernel, first, rows, pairs),
        in_specs=[SMEM] + [VMEM] * (2 * pairs) + [HBM] * len(before) + [ANY] * len(behind),
        out_specs=HBM,
        out_shape=jax.ShapeDtypeStruct((slots * rows, width), jnp.bfloat16),
        scratch_shapes=[pltpu.VMEM((total, width), jnp.bfloat16), pltpu.SemaphoreType.DMA((total // rows,))],
        input_output_aliases={1 + 2 * pairs: 0} if before else {},
        compiler_params=params(63),
        name="pack",
    )(sent, *own, *other, *before, *behind)


def list_places(peers, blocks):
    begin = peers * (SLOTS + SPILL)
    return begin, begin + blocks * PIECES + 1, begin + 2 * blocks * PIECES + 1


def list_kernel(rows, peers, blocks, *refs):
    sets, (plan_ref, more_ref, lines, values, table, codes, count, cross, sems) = refs[:4], refs[4:]
    me = lax.axis_index("sector")
    quarter = peers // 4
    chunk = SPILL * rows + INFO
    slots, targets = peers * SLOTS, blocks * PIECES
    begin_at, middle_at, where_at = list_places(peers, blocks)
    copies = []
    for which, ref in enumerate(sets):
        for z in range(quarter):
            i = which * quarter + z
            copies.append(pltpu.make_async_copy(ref.at[pl.ds(z * INFO, INFO)], lines.at[i], sems.at[i]))
            copies[-1].start()
    for i in range(targets + 1):
        count[i] = 0
    for i, copy in enumerate(copies):
        copy.wait()
        values[i : i + 1, :] = lines[i].astype(jnp.float32).astype(jnp.int32)[:1, :]
    copy = pltpu.make_async_copy(values, table, sems.at[peers])
    copy.start()
    copy.wait()

    def note(i, code):
        to = jnp.where(code >= 0, code, targets)
        codes[i] = to
        count[to] += 1

    def source(j, more):
        apart = j ^ me
        line = ((apart & 1) * 2 + ((apart >> 1) & 1)) * quarter + (apart >> 2)
        for slot in range(SLOTS):
            note(j * SLOTS + slot, table[line, me * SLOTS + slot])
        for i in range(SPILL):
            owner = table[j, slots + i]
            note(slots + j * SPILL + i, jnp.where(owner == me, table[j, slots + SPILL + i], -1))
        return jnp.maximum(more, table[j, TABLE - 1])

    more = lax.fori_loop(0, peers, source, 0, unroll=4)

    for i in range(peers):
        cross[i] = 0

    def passed(line, place):
        which, z = line // quarter, line % quarter
        origin = me ^ (z * 4 + which % 2 * 2 + which // 2)
        place = jnp.where(z == 0, 0, place)
        for j in range(SPILL):
            owner = table[line, slots + j]
            change = (owner >= 0) & ((owner ^ origin) & 2 == 2)
            to = jnp.maximum(owner, 0) // 4 * 4 + origin % 4
            cross[to] += change.astype(jnp.int32)
            plan_ref[where_at + line * SPILL + j] = place
            place = place + (change & (owner // 4 == me // 4)).astype(jnp.int32)
        return place

    lax.fori_loop(0, peers, passed, 0, unroll=4)
    for i in range(peers):
        more = jnp.maximum(more, (cross[i] > CROSS).astype(jnp.int32))
    more_ref[0] = more

    def total(t, before):
        plan_ref[begin_at + t] = before
        after = before + count[t]
        count[t] = before
        return after

    lax.fori_loop(0, targets + 1, total, 0, unroll=True)

    def put(i, _):
        code = codes[i]
        place = count[code]
        plan_ref[place] = i
        count[code] = place + 1
        return 0

    lax.fori_loop(0, slots, put, 0, unroll=peers // 2)
    for t in range(targets):
        plan_ref[middle_at + t] = count[t]
    lax.fori_loop(slots, slots + peers * SPILL, put, 0, unroll=peers // 2)


def land_kernel(rows, peers, plan_ref, arrived_ref, *refs):
    sets, (out_ref, held, stage, sems, out_sems) = refs[:4], refs[4:]
    quarter = peers // 4
    chunk = SPILL * rows + INFO
    slots = peers * SLOTS
    blocks, share, states = stage.shape
    begin_at, middle_at, where_at = list_places(peers, blocks)
    width = states // COL_PARTS

    def at(start, unit=rows):
        return pl.ds(pl.multiple_of(start, unit), rows)

    def fetch(i, ref, start):
        place = i - slots
        return pltpu.make_async_copy(ref.at[at(start, 16)], held.at[at(place * rows)], sems.at[place])

    def begin(n, _):
        i = plan_ref[n]

        @pl.when(i >= slots)
        def _():
            source, j = (i - slots) // SPILL, (i - slots) % SPILL
            for which in range(4):

                @pl.when(source // quarter == which)
                def _(which=which):
                    start = plan_ref[where_at + i - slots] * rows if which % 2 else source % quarter * chunk + j * rows
                    fetch(i, sets[which], start).start()

        return 0

    lax.fori_loop(0, plan_ref[begin_at + blocks * PIECES], begin, 0)

    copies = []
    half = PIECES // 2
    for t in range(blocks):
        for k in range(PIECES):
            g, c = k // COL_PARTS, k % COL_PARTS
            first, last = plan_ref[begin_at + t * PIECES + k], plan_ref[begin_at + t * PIECES + k + 1]
            place = (t, slice(g * rows, (g + 1) * rows), slice(c * width, (c + 1) * width))

            middle = plan_ref[middle_at + t * PIECES + k]
            alone = (last == first + 1) & (middle == last)

            @pl.when(alone)
            def _(place=place, first=first):
                stage[place] = arrived_ref[at(plan_ref[first] * rows), :]

            @pl.when(jnp.logical_not(alone))
            def _(place=place, first=first, middle=middle, last=last):
                def direct(n, total):
                    return total + arrived_ref[at(plan_ref[n] * rows), :].astype(jnp.float32)

                def spilled(n, total):
                    i = plan_ref[n]
                    fetch(i, sets[0], 0).wait()
                    return total + held[at((i - slots) * rows), :].astype(jnp.float32)

                total = lax.fori_loop(first, middle, direct, jnp.zeros((rows, width), jnp.float32))
                stage[place] = lax.fori_loop(middle, last, spilled, total).astype(stage.dtype)

            if k % half == half - 1:
                strip = pl.ds(k // half * (share // 2), share // 2)
                copies.append(pltpu.make_async_copy(stage.at[t, strip], out_ref.at[t, strip], out_sems.at[len(copies)]))
                copies[-1].start()
    for copy in copies:
        copy.wait()


def two_halves(wavefunction, left_env, right_env, mpo_mask, block_size, route_owner, route_block):
    blocks, states, _ = wavefunction.shape
    share = states // 2
    rows = share // ROW_GROUPS
    width = states // COL_PARTS
    peers = lax.axis_size("sector")
    chunk = SPILL * rows + INFO

    def bf16(*shape):
        return jax.ShapeDtypeStruct(shape, jnp.bfloat16)

    def int32(*shape):
        return jax.ShapeDtypeStruct(shape, jnp.int32)

    def swap(x):
        return lax.ppermute(x, "mpo", [(0, 1), (1, 0)])

    def across(x, apart):
        return lax.ppermute(x, "sector", [(i, i ^ apart) for i in range(peers)])

    own, send, other = [], [], []

    def run(first, count, plan, behind):
        made = terms(first, count, block_size, mpo_mask, wavefunction, left_env[0], right_env[0], plan, behind)
        for n in range(count):
            own.append(made[2 * n])
            send.append(made[2 * n + 1])
            other.append(swap(send[-1]))
        return made[2 * count :]

    for b in range(SPILL_BLOCKS):
        tables = run(b, 1, [route_owner, route_block] if b == SPILL_BLOCKS - 1 else [], send[-1:])
    sent, info = tables
    run(SPILL_BLOCKS, blocks - SPILL_BLOCKS, [], send[-1:])

    spilled = pl.pallas_call(
        functools.partial(spill_kernel, rows, blocks),
        in_specs=[SMEM, VMEM] + [HBM] * (2 * SPILL_BLOCKS) + [ANY],
        out_specs=VMEM,
        out_shape=bf16(chunk, width),
        scratch_shapes=[pltpu.VMEM((SPILL * rows, width), jnp.bfloat16)] * 2
        + [pltpu.SemaphoreType.DMA((SPILL,))] * 2,
        compiler_params=params(63),
        name="spill",
    )(sent, info.reshape(1, TABLE), *own[:SPILL_BLOCKS], *other[:SPILL_BLOCKS], send[-1])
    last = blocks - 1
    along = [across(spilled, apart) for apart in range(4, peers, 4)]
    packed = pack(0, sent, own[:last], other[:last], None, rows, peers * SLOTS, [])
    packed = pack(last, sent, own[last:], other[last:], packed, rows, peers * SLOTS, [])
    near, tables, crossing = join(rows, peers, [packed], spilled, *along)
    tables_beside, tables_mate = across(tables, 2), across(tables, 1)
    tables = [tables, tables_beside, tables_mate, across(tables_beside, 1)]
    beside = across(crossing, 2)
    arrived = lax.all_to_all(packed.reshape(peers, SLOTS * rows, width), "sector", split_axis=0, concat_axis=0, tiled=True)
    arrived = arrived.reshape(peers * SLOTS * rows, width)

    pieces = peers * (SLOTS + SPILL)
    plan, more = pl.pallas_call(
        functools.partial(list_kernel, rows, peers, blocks),
        in_specs=[HBM] * 4,
        out_specs=[SMEM] * 2,
        out_shape=[int32(list_places(peers, blocks)[-1] + peers * SPILL), int32(1)],
        scratch_shapes=[
            pltpu.VMEM((peers, INFO, TABLE), jnp.bfloat16),
            pltpu.VMEM((peers, TABLE), jnp.int32),
            pltpu.SMEM((peers, TABLE), jnp.int32),
            pltpu.SMEM((pieces,), jnp.int32),
            pltpu.SMEM((blocks * PIECES + 1,), jnp.int32),
            pltpu.SMEM((peers,), jnp.int32),
            pltpu.SemaphoreType.DMA((peers + 1,)),
        ],
        compiler_params=params(16),
        cost_estimate=pl.CostEstimate(flops=17000000000, bytes_accessed=0, transcendentals=0),
        name="list",
    )(*tables)

    more = jnp.maximum(more, swap(more))
    beside, plan, more = lax.optimization_barrier((beside, plan, more))
    sets = [near, beside, across(near, 1), across(beside, 1)]

    def fast(plan, arrived, sets, *_):
        return pl.pallas_call(
            functools.partial(land_kernel, rows, peers),
            in_specs=[SMEM, VMEM] + [ANY] * 4,
            out_specs=HBM,
            out_shape=bf16(blocks, share, states),
            scratch_shapes=[
                pltpu.VMEM((peers * SPILL * rows, width), jnp.bfloat16),
                pltpu.VMEM((blocks, share, states), jnp.bfloat16),
                pltpu.SemaphoreType.DMA((peers * SPILL,)),
                pltpu.SemaphoreType.DMA((2 * blocks,)),
            ],
            compiler_params=params(16),
            name="land",
        )(plan, arrived, *sets)

    def slow(landed, own, other):
        sums = jnp.concatenate([add(a, b[: a.shape[0]]) for a, b in zip(own, other)], axis=0)
        sums = sums.reshape(blocks, ROW_GROUPS, COL_PARTS, rows, width).transpose(1, 3, 0, 2, 4)
        return exchange_all(sums.reshape(share, blocks, states), route_owner, route_block)

    landed = fast(plan, arrived, tuple(sets))
    return lax.cond(more[0] <= 0, lambda landed, own, other: landed, slow, landed, tuple(own), tuple(other))


def solution(mesh):
    placed = (
        P("sector", None, None),
        P("mpo", "sector", None, None),
        P("mpo", "sector", None, None),
        P("mpo", "sector"),
        P("sector"),
        P("mpo", "sector", None),
        P("mpo", "sector", None),
    )

    def per_device(wavefunction, *rest):
        states = wavefunction.shape[1]
        peers = mesh.shape["sector"]
        fits = (
            mesh.shape["mpo"] == 2
            and peers >= 8
            and peers & (peers - 1) == 0
            and wavefunction.shape[0] == SLOTS + SPILL_BLOCKS
            and states // COL_PARTS == TABLE
            and states // (2 * ROW_GROUPS) % 16 == 0
            and peers * SLOTS + 2 * SPILL < TABLE
        )
        return (two_halves if fits else general)(wavefunction, *rest)

    return jax.shard_map(per_device, mesh=mesh, in_specs=placed, out_specs=P("sector", "mpo", None), check_vma=False)
```

```python
import functools

import jax
import jax.numpy as jnp
from jax import lax
from jax.experimental import pallas as pl
from jax.experimental.pallas import tpu as pltpu
from jax.sharding import PartitionSpec as P

ROW_GROUPS = 4
COL_PARTS = 2
PIECES = 8
SLOTS = 2
SPILL = 3
SPILL_BLOCKS = 2
CROSS = 8
INFO = 16
TABLE = 256

VMEM = pl.BlockSpec(memory_space=pltpu.VMEM)
SMEM = pl.BlockSpec(memory_space=pltpu.SMEM)
ANY = pl.BlockSpec(memory_space=pl.ANY)
HBM = pl.BlockSpec(memory_space=pltpu.HBM)


def params(mib):
    return pltpu.CompilerParams(vmem_limit_bytes=mib * 2**20)


def exchange_all(sigma_share, route_owner, route_block):
    row_count, block_count, states = sigma_share.shape
    group_rows = row_count // ROW_GROUPS
    width_part = states // COL_PARTS
    pieces = sigma_share.reshape(ROW_GROUPS, group_rows, block_count, COL_PARTS, width_part)
    pieces = pieces.transpose(2, 0, 3, 1, 4).reshape(block_count * PIECES, group_rows * width_part)
    owners = route_owner[0].reshape(-1)
    target_code = (route_block[0] * PIECES + jnp.arange(PIECES, dtype=jnp.int32)[None, :]).reshape(-1)
    peer_count = lax.axis_size("sector")
    capacity = min(block_count, max(2, (2 * block_count * PIECES + peer_count - 1) // peer_count))
    is_owner = (owners[:, None] == jnp.arange(peer_count, dtype=jnp.int32)[None, :]).astype(jnp.int32)
    before = jnp.cumsum(is_owner, axis=0) - is_owner
    position = jnp.sum(before * is_owner, axis=1)
    destination = owners * capacity + position
    slot_ids = jnp.arange(peer_count * capacity, dtype=jnp.int32)
    placing = slot_ids[:, None] == destination[None, :]
    send_data = jnp.dot(placing.astype(jnp.bfloat16), pieces, preferred_element_type=jnp.float32).astype(jnp.bfloat16)
    send_data = send_data.reshape(peer_count, capacity, group_rows * width_part)
    send_code = (jnp.sum(placing.astype(jnp.int32) * (target_code + 1)[None, :], axis=1) - 1).reshape(peer_count, capacity)
    arrived_data, arrived_code = (
        lax.all_to_all(send_data, "sector", split_axis=0, concat_axis=0, tiled=True),
        lax.all_to_all(send_code, "sector", split_axis=0, concat_axis=0, tiled=True),
    )
    arrived_data = arrived_data.reshape(peer_count * capacity, group_rows * width_part)
    arrived_code = arrived_code.reshape(-1)
    targets = jnp.arange(block_count * PIECES, dtype=jnp.int32)
    collect = (arrived_code[None, :] == targets[:, None]).astype(jnp.bfloat16)
    landed = jnp.dot(collect, arrived_data, preferred_element_type=jnp.float32).astype(jnp.bfloat16)
    landed = landed.reshape(block_count, ROW_GROUPS, COL_PARTS, group_rows, width_part)
    return landed.transpose(0, 1, 3, 2, 4).reshape(block_count, row_count, states)


def general(wavefunction, left_env, right_env, mpo_mask, block_size, route_owner, route_block):
    states = wavefunction.shape[1]
    row_count = states // lax.axis_size("mpo")
    positions = jnp.arange(states, dtype=jnp.int32)
    live_cols = positions[None, :] < block_size[:, None]
    live_mask = live_cols[:, :, None] & live_cols[:, None, :]
    masked = jnp.where(live_mask, wavefunction, jnp.zeros_like(wavefunction))
    right_part = jnp.einsum("bij,bkj->bik", masked, right_env[0], preferred_element_type=jnp.float32).astype(jnp.bfloat16)
    factor = mpo_mask[0].astype(jnp.float32)
    product = jnp.einsum("bij,bjk->ibk", left_env[0], right_part, preferred_element_type=jnp.float32)
    row_share = lax.psum_scatter(
        (product * factor[None, :, None]).astype(jnp.bfloat16), "mpo", scatter_dimension=0, tiled=True
    ).astype(jnp.float32)
    global_rows = lax.axis_index("mpo") * row_count + jnp.arange(row_count, dtype=jnp.int32)
    live_rows = global_rows[:, None] < block_size[None, :]
    share_mask = live_rows[:, :, None] & live_cols[None, :, :]
    sigma_share = jnp.where(share_mask, row_share, jnp.zeros_like(row_share)).astype(jnp.bfloat16)
    return exchange_all(sigma_share, route_owner, route_block)


def route(peers, blocks, group_rows, width, owner_ref, block_ref, size_ref, sent_ref, info_ref, count):
    first_row = lax.axis_index("mpo") * (ROW_GROUPS * group_rows)
    spill_at = peers * SLOTS
    for i in range(spill_at + 2 * SPILL):
        info_ref[i] = -1
    for i in range(SPILL):
        sent_ref[blocks * PIECES + i] = -1
    for i in range(peers):
        count[i] = 0

    nowhere = TABLE - 2

    def one(step, spilled):
        b, k = blocks - 1 - step // PIECES, step % PIECES
        i = b * PIECES + k
        g, c = k // COL_PARTS, k % COL_PARTS
        size = size_ref[b]
        live = (first_row + g * group_rows < size) & (c * width < size)
        owner = owner_ref[0, b, k]
        pos = count[owner]
        code = block_ref[0, b, k] * PIECES + k
        direct = live & (pos < SLOTS)
        kept = live & (pos >= SLOTS) & (spilled < SPILL)
        sent_ref[i] = jnp.where(direct, owner * SLOTS + pos, -1)
        info_ref[jnp.where(direct, owner * SLOTS + pos, nowhere)] = code
        count[owner] = pos + direct.astype(jnp.int32)
        sent_ref[jnp.where(kept, blocks * PIECES + spilled, nowhere)] = i
        info_ref[jnp.where(kept, spill_at + spilled, nowhere)] = owner
        info_ref[jnp.where(kept, spill_at + SPILL + spilled, nowhere)] = code
        return spilled + (live & (pos >= SLOTS)).astype(jnp.int32)

    spilled = lax.fori_loop(0, blocks * PIECES, one, 0, unroll=PIECES)
    sent_ref[TABLE - 1] = (spilled > SPILL).astype(jnp.int32)


def term_kernel(first, plan, size_ref, mask_ref, wave_ref, left_ref, right_ref, *refs):
    tables = ()
    if plan:
        tables = (*refs[:2], size_ref, *refs[-10:-8], refs[-1])
        refs = refs[2:-10] + refs[-8:-1]
    wave, left, right, own, send, come, go = refs[-7:]
    results = refs[-7 - 2 * wave.shape[0] : -7]
    count, states, _ = wave.shape
    share = states // 2
    rows, width = share // ROW_GROUPS, states // COL_PARTS
    mine = lax.axis_index("mpo").astype(jnp.int32)
    arrive = []
    for n in range(count):
        arrive.append(
            [
                pltpu.make_async_copy(source.at[first + n], target.at[n], come.at[n, i])
                for i, (source, target) in enumerate(((wave_ref, wave), (right_ref, right), (left_ref, left)))
            ]
        )
        for copy in arrive[-1]:
            copy.start()
    leave = []
    if plan:
        route(*plan, *tables)
    row = lax.broadcasted_iota(jnp.int32, (states, states), 0)
    col = lax.broadcasted_iota(jnp.int32, (states, states), 1)
    for n in range(count):
        size = size_ref[first + n]
        active = mask_ref[0, first + n] != 0
        arrive[n][0].wait()
        masked = jnp.where((row < size) & (col < size), wave[n], jnp.zeros_like(wave[n]))
        arrive[n][1].wait()
        part = lax.dot_general(masked, right[n], (((1,), (1,)), ((), ())), preferred_element_type=jnp.float32)
        part = part.astype(jnp.bfloat16)
        arrive[n][2].wait()
        for which, (target, out_ref, half) in enumerate(((send, results[2 * n + 1], 1 - mine), (own, results[2 * n], mine))):
            start = pl.multiple_of(half * share, share)
            product = jnp.dot(left[n, pl.ds(start, share), :], part, preferred_element_type=jnp.float32)
            keep = (row[:share] + start < size) & (col[:share] < size) & active
            product = jnp.where(keep, product, 0.0).astype(jnp.bfloat16)
            for k in range(PIECES):
                g, c = k // COL_PARTS, k % COL_PARTS
                target[n, k * rows : (k + 1) * rows, :] = product[g * rows : (g + 1) * rows, c * width : (c + 1) * width]
            leave.append(pltpu.make_async_copy(target.at[n], out_ref, go.at[n, which]))
            leave[-1].start()
    for copy in leave:
        copy.wait()


def terms(first, count, sizes, mask, wave, left, right, plan, behind):
    blocks, states, _ = wave.shape
    group_rows, width = states // 2 // ROW_GROUPS, states // COL_PARTS
    rows = PIECES * group_rows
    out = jax.ShapeDtypeStruct((rows, width), jnp.bfloat16)
    table = jax.ShapeDtypeStruct((TABLE,), jnp.int32)
    peers = lax.axis_size("sector")
    scratch = [pltpu.VMEM((count, states, states), jnp.bfloat16)] * 3 + [pltpu.VMEM((count, rows, width), jnp.bfloat16)] * 2
    scratch += [pltpu.SemaphoreType.DMA((count, 3)), pltpu.SemaphoreType.DMA((count, 2))]
    if plan:
        scratch += [pltpu.SMEM((peers,), jnp.int32)]
    return pl.pallas_call(
        functools.partial(term_kernel, first, (peers, blocks, group_rows, width) if plan else None),
        in_specs=[SMEM] * 2 + [HBM] * 3 + [SMEM] * len(plan) + [ANY] * len(behind),
        out_specs=[HBM] * (2 * count) + [SMEM] * len(plan),
        out_shape=[out] * (2 * count) + [table] * len(plan),
        scratch_shapes=scratch,
        compiler_params=params(63),
        cost_estimate=pl.CostEstimate(flops=3000000000, bytes_accessed=1, transcendentals=0),
        name="terms",
    )(sizes, mask, wave, left, right, *plan, *behind)


def add(a, b):
    return (a.astype(jnp.float32) + b.astype(jnp.float32)).astype(jnp.bfloat16)


def fetch_spill(rows, blocks, sent_ref, sources, target, sems):
    for j in range(SPILL):
        index = sent_ref[blocks * PIECES + j]
        for b in range(SPILL_BLOCKS):

            def copy(b=b, j=j, index=index):
                at = pl.ds(pl.multiple_of((index - b * PIECES) * rows, rows), rows)
                return pltpu.make_async_copy(sources[b].at[at], target.at[pl.ds(j * rows, rows)], sems.at[j])

            yield (index >= b * PIECES) & (index < (b + 1) * PIECES), copy


def run_copies(copies):
    copies = list(copies)
    for step in ("start", "wait"):
        for there, copy in copies:

            @pl.when(there)
            def _(copy=copy, step=step):
                getattr(copy(), step)()


def spill_kernel(rows, blocks, sent_ref, info_ref, *refs):
    own_refs, other_refs = refs[:SPILL_BLOCKS], refs[SPILL_BLOCKS : 2 * SPILL_BLOCKS]
    out_ref, own, other, own_sems, other_sems = refs[2 * SPILL_BLOCKS + 1 :]
    run_copies(
        [*fetch_spill(rows, blocks, sent_ref, own_refs, own, own_sems), *fetch_spill(rows, blocks, sent_ref, other_refs, other, other_sems)]
    )
    out_ref[: SPILL * rows, :] = add(own[...], other[...])
    lane = lax.broadcasted_iota(jnp.int32, (INFO, TABLE), 1)
    table = jnp.where(lane == TABLE - 1, sent_ref[TABLE - 1], info_ref[...])
    out_ref[SPILL * rows :, :] = table.astype(jnp.float32).astype(jnp.bfloat16)


def join_kernel(rows, peers, count, *refs):
    near_ref, tables_ref, cross_ref, held, values, table, come, go = refs[-8:]
    me = lax.axis_index("sector").astype(jnp.int32)
    chunk = refs[0].shape[0]
    spill_at = peers * SLOTS
    arrive = [pltpu.make_async_copy(ref, held.at[pl.ds(i * chunk, chunk)], come.at[i]) for i, ref in enumerate(refs[:count])]
    for copy in arrive:
        copy.start()
    leave = []
    for i, copy in enumerate(arrive):
        copy.wait()
        at, info = pl.ds(i * chunk, chunk), pl.ds((i + 1) * chunk - INFO, INFO)
        leave.append(pltpu.make_async_copy(held.at[info], tables_ref.at[pl.ds(i * INFO, INFO)], go.at[count + i]))
        leave.append(pltpu.make_async_copy(held.at[at], near_ref.at[at], go.at[i]))
        leave[-2].start()
        leave[-1].start()
        values[i : i + 1, :] = held[(i + 1) * chunk - INFO : (i + 1) * chunk, :].astype(jnp.float32).astype(jnp.int32)[:1, :]
    copy = pltpu.make_async_copy(values, table, go.at[2 * count])
    copy.start()
    copy.wait()
    moves = []
    place = 0
    for i in range(count):
        for j in range(SPILL):
            owner = table[i, spill_at + j]
            there = (owner >= 0) & (owner // 4 == me // 4) & ((owner ^ me) & 2 == 2)
            fits = there & (place < CROSS)

            def move(i=i, j=j, place=place):
                to = pl.ds(pl.multiple_of(place * rows, rows), rows)
                sem = go.at[2 * count + 1 + i * SPILL + j]
                return pltpu.make_async_copy(held.at[pl.ds(i * chunk + j * rows, rows)], cross_ref.at[to], sem)

            moves.append((fits, move))
            place = place + there.astype(jnp.int32)
    run_copies(moves)
    for copy in leave:
        copy.wait()


def join(rows, peers, behind, *parts):
    chunk, width = parts[0].shape
    count = len(parts)
    return pl.pallas_call(
        functools.partial(join_kernel, rows, peers, count),
        in_specs=[ANY] * (count + len(behind)),
        out_specs=[HBM] * 3,
        out_shape=[jax.ShapeDtypeStruct((n, width), jnp.bfloat16) for n in (count * chunk, count * INFO, CROSS * rows)],
        scratch_shapes=[
            pltpu.VMEM((count * chunk, width), jnp.bfloat16),
            pltpu.VMEM((count, TABLE), jnp.int32),
            pltpu.SMEM((count, TABLE), jnp.int32),
            pltpu.SemaphoreType.DMA((count,)),
            pltpu.SemaphoreType.DMA((2 * count + 1 + count * SPILL,)),
        ],
        compiler_params=params(16),
        name="join",
    )(*parts, *behind)


def pack_kernel(first, rows, pairs, sent_ref, *refs):
    own_refs, other_refs = refs[:pairs], refs[pairs : 2 * pairs]
    out_ref, stage, sems = refs[-3:]
    done = 0
    copies = []
    for own_ref, other_ref in zip(own_refs, other_refs):
        count = own_ref.shape[0] // rows
        stage[done * rows : (done + count) * rows, :] = add(own_ref[...], other_ref[: count * rows, :])
        for k in range(done, done + count):
            slot = sent_ref[first * PIECES + k]

            def copy(k=k, slot=slot):
                to = pl.ds(pl.multiple_of(slot * rows, rows), rows)
                return pltpu.make_async_copy(stage.at[pl.ds(k * rows, rows)], out_ref.at[to], sems.at[k])

            copies.append((slot >= 0, copy))

            @pl.when(slot >= 0)
            def _(copy=copy):
                copy().start()

        done += count
    for there, copy in copies:

        @pl.when(there)
        def _(copy=copy):
            copy().wait()


def pack(first, sent, own, other, packed, rows, slots, behind):
    total, width = sum(x.shape[0] for x in own), own[0].shape[1]
    before = [] if packed is None else [packed]
    pairs = len(own)
    return pl.pallas_call(
        functools.partial(pack_kernel, first, rows, pairs),
        in_specs=[SMEM] + [VMEM] * (2 * pairs) + [HBM] * len(before) + [ANY] * len(behind),
        out_specs=HBM,
        out_shape=jax.ShapeDtypeStruct((slots * rows, width), jnp.bfloat16),
        scratch_shapes=[pltpu.VMEM((total, width), jnp.bfloat16), pltpu.SemaphoreType.DMA((total // rows,))],
        input_output_aliases={1 + 2 * pairs: 0} if before else {},
        compiler_params=params(63),
        name="pack",
    )(sent, *own, *other, *before, *behind)


def list_places(peers, blocks):
    begin = peers * (SLOTS + SPILL)
    return begin, begin + blocks * PIECES + 1, begin + 2 * blocks * PIECES + 1


def list_kernel(rows, peers, blocks, *refs):
    sets, (plan_ref, more_ref, lines, values, table, codes, count, cross, sems) = refs[:4], refs[4:]
    me = lax.axis_index("sector")
    quarter = peers // 4
    chunk = SPILL * rows + INFO
    slots, targets = peers * SLOTS, blocks * PIECES
    begin_at, middle_at, where_at = list_places(peers, blocks)
    copies = []
    for which, ref in enumerate(sets):
        for z in range(quarter):
            i = which * quarter + z
            copies.append(pltpu.make_async_copy(ref.at[pl.ds(z * INFO, INFO)], lines.at[i], sems.at[i]))
            copies[-1].start()
    for i in range(targets + 1):
        count[i] = 0
    for i, copy in enumerate(copies):
        copy.wait()
        values[i : i + 1, :] = lines[i].astype(jnp.float32).astype(jnp.int32)[:1, :]
    copy = pltpu.make_async_copy(values, table, sems.at[peers])
    copy.start()
    copy.wait()

    def note(i, code):
        to = jnp.where(code >= 0, code, targets)
        codes[i] = to
        count[to] += 1

    def source(j, more):
        apart = j ^ me
        line = ((apart & 1) * 2 + ((apart >> 1) & 1)) * quarter + (apart >> 2)
        for slot in range(SLOTS):
            note(j * SLOTS + slot, table[line, me * SLOTS + slot])
        for i in range(SPILL):
            owner = table[j, slots + i]
            note(slots + j * SPILL + i, jnp.where(owner == me, table[j, slots + SPILL + i], -1))
        return jnp.maximum(more, table[j, TABLE - 1])

    more = lax.fori_loop(0, peers, source, 0, unroll=4)

    for i in range(peers):
        cross[i] = 0

    def passed(line, place):
        which, z = line // quarter, line % quarter
        origin = me ^ (z * 4 + which % 2 * 2 + which // 2)
        place = jnp.where(z == 0, 0, place)
        for j in range(SPILL):
            owner = table[line, slots + j]
            change = (owner >= 0) & ((owner ^ origin) & 2 == 2)
            to = jnp.maximum(owner, 0) // 4 * 4 + origin % 4
            cross[to] += change.astype(jnp.int32)
            plan_ref[where_at + line * SPILL + j] = place
            place = place + (change & (owner // 4 == me // 4)).astype(jnp.int32)
        return place

    lax.fori_loop(0, peers, passed, 0, unroll=4)
    for i in range(peers):
        more = jnp.maximum(more, (cross[i] > CROSS).astype(jnp.int32))
    more_ref[0] = more

    def total(t, before):
        plan_ref[begin_at + t] = before
        after = before + count[t]
        count[t] = before
        return after

    lax.fori_loop(0, targets + 1, total, 0, unroll=True)

    def put(i, _):
        code = codes[i]
        place = count[code]
        plan_ref[place] = i
        count[code] = place + 1
        return 0

    lax.fori_loop(0, slots, put, 0, unroll=peers // 2)
    for t in range(targets):
        plan_ref[middle_at + t] = count[t]
    lax.fori_loop(slots, slots + peers * SPILL, put, 0, unroll=peers // 2)


def land_kernel(rows, peers, plan_ref, arrived_ref, *refs):
    sets, (out_ref, held, stage, sems, out_sems) = refs[:4], refs[4:]
    quarter = peers // 4
    chunk = SPILL * rows + INFO
    slots = peers * SLOTS
    blocks, share, states = stage.shape
    begin_at, middle_at, where_at = list_places(peers, blocks)
    width = states // COL_PARTS

    def at(start, unit=rows):
        return pl.ds(pl.multiple_of(start, unit), rows)

    def fetch(i, ref, start):
        place = i - slots
        return pltpu.make_async_copy(ref.at[at(start, 16)], held.at[at(place * rows)], sems.at[place])

    def begin(n, _):
        i = plan_ref[n]

        @pl.when(i >= slots)
        def _():
            source, j = (i - slots) // SPILL, (i - slots) % SPILL
            for which in range(4):

                @pl.when(source // quarter == which)
                def _(which=which):
                    place = jnp.minimum(plan_ref[where_at + i - slots], CROSS - 1)
                    start = place * rows if which % 2 else source % quarter * chunk + j * rows
                    fetch(i, sets[which], start).start()

        return 0

    lax.fori_loop(0, plan_ref[begin_at + blocks * PIECES], begin, 0)

    copies = []
    half = PIECES // 2
    for t in range(blocks):
        for k in range(PIECES):
            g, c = k // COL_PARTS, k % COL_PARTS
            first, last = plan_ref[begin_at + t * PIECES + k], plan_ref[begin_at + t * PIECES + k + 1]
            place = (t, slice(g * rows, (g + 1) * rows), slice(c * width, (c + 1) * width))

            middle = plan_ref[middle_at + t * PIECES + k]
            alone = (last == first + 1) & (middle == last)

            @pl.when(alone)
            def _(place=place, first=first):
                stage[place] = arrived_ref[at(plan_ref[first] * rows), :]

            @pl.when(jnp.logical_not(alone))
            def _(place=place, first=first, middle=middle, last=last):
                def direct(n, total):
                    return total + arrived_ref[at(plan_ref[n] * rows), :].astype(jnp.float32)

                def spilled(n, total):
                    i = plan_ref[n]
                    fetch(i, sets[0], 0).wait()
                    return total + held[at((i - slots) * rows), :].astype(jnp.float32)

                total = lax.fori_loop(first, middle, direct, jnp.zeros((rows, width), jnp.float32))
                stage[place] = lax.fori_loop(middle, last, spilled, total).astype(stage.dtype)

            if k % half == half - 1:
                strip = pl.ds(k // half * (share // 2), share // 2)
                copies.append(pltpu.make_async_copy(stage.at[t, strip], out_ref.at[t, strip], out_sems.at[len(copies)]))
                copies[-1].start()
    for copy in copies:
        copy.wait()


def two_halves(wavefunction, left_env, right_env, mpo_mask, block_size, route_owner, route_block):
    blocks, states, _ = wavefunction.shape
    share = states // 2
    rows = share // ROW_GROUPS
    width = states // COL_PARTS
    peers = lax.axis_size("sector")
    chunk = SPILL * rows + INFO

    def bf16(*shape):
        return jax.ShapeDtypeStruct(shape, jnp.bfloat16)

    def int32(*shape):
        return jax.ShapeDtypeStruct(shape, jnp.int32)

    def swap(x):
        return lax.ppermute(x, "mpo", [(0, 1), (1, 0)])

    def across(x, apart):
        return lax.ppermute(x, "sector", [(i, i ^ apart) for i in range(peers)])

    own, send, other = [], [], []

    def run(first, count, plan, behind):
        made = terms(first, count, block_size, mpo_mask, wavefunction, left_env[0], right_env[0], plan, behind)
        for n in range(count):
            own.append(made[2 * n])
            send.append(made[2 * n + 1])
            other.append(swap(send[-1]))
        return made[2 * count :]

    for b in range(SPILL_BLOCKS):
        tables = run(b, 1, [route_owner, route_block] if b == SPILL_BLOCKS - 1 else [], send[-1:])
    sent, info = tables
    run(SPILL_BLOCKS, blocks - SPILL_BLOCKS, [], send[-1:])

    spilled = pl.pallas_call(
        functools.partial(spill_kernel, rows, blocks),
        in_specs=[SMEM, VMEM] + [HBM] * (2 * SPILL_BLOCKS) + [ANY],
        out_specs=VMEM,
        out_shape=bf16(chunk, width),
        scratch_shapes=[pltpu.VMEM((SPILL * rows, width), jnp.bfloat16)] * 2
        + [pltpu.SemaphoreType.DMA((SPILL,))] * 2,
        compiler_params=params(63),
        name="spill",
    )(sent, info.reshape(1, TABLE), *own[:SPILL_BLOCKS], *other[:SPILL_BLOCKS], send[-1])
    last = blocks - 1
    along = [across(spilled, apart) for apart in range(4, peers, 4)]
    packed = pack(0, sent, own[:last], other[:last], None, rows, peers * SLOTS, [])
    packed = pack(last, sent, own[last:], other[last:], packed, rows, peers * SLOTS, [])
    near, tables, crossing = join(rows, peers, [packed], spilled, *along)
    tables_beside, tables_mate = across(tables, 2), across(tables, 1)
    tables = [tables, tables_beside, tables_mate, across(tables_beside, 1)]
    beside = across(crossing, 2)
    arrived = lax.all_to_all(packed.reshape(peers, SLOTS * rows, width), "sector", split_axis=0, concat_axis=0, tiled=True)
    arrived = arrived.reshape(peers * SLOTS * rows, width)

    pieces = peers * (SLOTS + SPILL)
    plan, more = pl.pallas_call(
        functools.partial(list_kernel, rows, peers, blocks),
        in_specs=[HBM] * 4,
        out_specs=[SMEM] * 2,
        out_shape=[int32(list_places(peers, blocks)[-1] + peers * SPILL), int32(1)],
        scratch_shapes=[
            pltpu.VMEM((peers, INFO, TABLE), jnp.bfloat16),
            pltpu.VMEM((peers, TABLE), jnp.int32),
            pltpu.SMEM((peers, TABLE), jnp.int32),
            pltpu.SMEM((pieces,), jnp.int32),
            pltpu.SMEM((blocks * PIECES + 1,), jnp.int32),
            pltpu.SMEM((peers,), jnp.int32),
            pltpu.SemaphoreType.DMA((peers + 1,)),
        ],
        compiler_params=params(16),
        cost_estimate=pl.CostEstimate(flops=17000000000, bytes_accessed=0, transcendentals=0),
        name="list",
    )(*tables)

    more = jnp.maximum(more, swap(more))
    beside, plan, more = lax.optimization_barrier((beside, plan, more))
    sets = [near, beside, across(near, 1), across(beside, 1)]

    def fast(plan, arrived, sets, *_):
        return pl.pallas_call(
            functools.partial(land_kernel, rows, peers),
            in_specs=[SMEM, VMEM] + [ANY] * 4,
            out_specs=HBM,
            out_shape=bf16(blocks, share, states),
            scratch_shapes=[
                pltpu.VMEM((peers * SPILL * rows, width), jnp.bfloat16),
                pltpu.VMEM((blocks, share, states), jnp.bfloat16),
                pltpu.SemaphoreType.DMA((peers * SPILL,)),
                pltpu.SemaphoreType.DMA((2 * blocks,)),
            ],
            compiler_params=params(16),
            name="land",
        )(plan, arrived, *sets)

    def slow(landed, own, other):
        sums = jnp.concatenate([add(a, b[: a.shape[0]]) for a, b in zip(own, other)], axis=0)
        sums = sums.reshape(blocks, ROW_GROUPS, COL_PARTS, rows, width).transpose(1, 3, 0, 2, 4)
        return exchange_all(sums.reshape(share, blocks, states), route_owner, route_block)

    landed = fast(plan, arrived, tuple(sets))
    return lax.cond(more[0] <= 0, lambda landed, own, other: landed, slow, landed, tuple(own), tuple(other))


def solution(mesh):
    placed = (
        P("sector", None, None),
        P("mpo", "sector", None, None),
        P("mpo", "sector", None, None),
        P("mpo", "sector"),
        P("sector"),
        P("mpo", "sector", None),
        P("mpo", "sector", None),
    )

    def per_device(wavefunction, *rest):
        states = wavefunction.shape[1]
        peers = mesh.shape["sector"]
        fits = (
            mesh.shape["mpo"] == 2
            and peers >= 8
            and peers & (peers - 1) == 0
            and wavefunction.shape[0] == SLOTS + SPILL_BLOCKS
            and states // COL_PARTS == TABLE
            and states // (2 * ROW_GROUPS) % 16 == 0
            and peers * SLOTS + 2 * SPILL < TABLE
        )
        return (two_halves if fits else general)(wavefunction, *rest)

    return jax.shard_map(per_device, mesh=mesh, in_specs=placed, out_specs=P("sector", "mpo", None), check_vma=False)
```

```python
import functools

import jax
import jax.numpy as jnp
from jax import lax
from jax.experimental import pallas as pl
from jax.experimental.pallas import tpu as pltpu
from jax.sharding import PartitionSpec as P

ROW_GROUPS = 4
COL_PARTS = 2
PIECES = 8
SLOTS = 2
SPILL = 3
SPILL_BLOCKS = 2
CROSS = 8
INFO = 16
TABLE = 256

VMEM = pl.BlockSpec(memory_space=pltpu.VMEM)
SMEM = pl.BlockSpec(memory_space=pltpu.SMEM)
ANY = pl.BlockSpec(memory_space=pl.ANY)
HBM = pl.BlockSpec(memory_space=pltpu.HBM)


def params(mib):
    return pltpu.CompilerParams(vmem_limit_bytes=mib * 2**20)


def exchange_all(sigma_share, route_owner, route_block):
    row_count, block_count, states = sigma_share.shape
    group_rows = row_count // ROW_GROUPS
    width_part = states // COL_PARTS
    pieces = sigma_share.reshape(ROW_GROUPS, group_rows, block_count, COL_PARTS, width_part)
    pieces = pieces.transpose(2, 0, 3, 1, 4).reshape(block_count * PIECES, group_rows * width_part)
    owners = route_owner[0].reshape(-1)
    target_code = (route_block[0] * PIECES + jnp.arange(PIECES, dtype=jnp.int32)[None, :]).reshape(-1)
    peer_count = lax.axis_size("sector")
    capacity = min(block_count, max(2, (2 * block_count * PIECES + peer_count - 1) // peer_count))
    is_owner = (owners[:, None] == jnp.arange(peer_count, dtype=jnp.int32)[None, :]).astype(jnp.int32)
    before = jnp.cumsum(is_owner, axis=0) - is_owner
    position = jnp.sum(before * is_owner, axis=1)
    destination = owners * capacity + position
    slot_ids = jnp.arange(peer_count * capacity, dtype=jnp.int32)
    placing = slot_ids[:, None] == destination[None, :]
    send_data = jnp.dot(placing.astype(jnp.bfloat16), pieces, preferred_element_type=jnp.float32).astype(jnp.bfloat16)
    send_data = send_data.reshape(peer_count, capacity, group_rows * width_part)
    send_code = (jnp.sum(placing.astype(jnp.int32) * (target_code + 1)[None, :], axis=1) - 1).reshape(peer_count, capacity)
    arrived_data, arrived_code = (
        lax.all_to_all(send_data, "sector", split_axis=0, concat_axis=0, tiled=True),
        lax.all_to_all(send_code, "sector", split_axis=0, concat_axis=0, tiled=True),
    )
    arrived_data = arrived_data.reshape(peer_count * capacity, group_rows * width_part)
    arrived_code = arrived_code.reshape(-1)
    targets = jnp.arange(block_count * PIECES, dtype=jnp.int32)
    collect = (arrived_code[None, :] == targets[:, None]).astype(jnp.bfloat16)
    landed = jnp.dot(collect, arrived_data, preferred_element_type=jnp.float32).astype(jnp.bfloat16)
    landed = landed.reshape(block_count, ROW_GROUPS, COL_PARTS, group_rows, width_part)
    return landed.transpose(0, 1, 3, 2, 4).reshape(block_count, row_count, states)


def general(wavefunction, left_env, right_env, mpo_mask, block_size, route_owner, route_block):
    states = wavefunction.shape[1]
    row_count = states // lax.axis_size("mpo")
    positions = jnp.arange(states, dtype=jnp.int32)
    live_cols = positions[None, :] < block_size[:, None]
    live_mask = live_cols[:, :, None] & live_cols[:, None, :]
    masked = jnp.where(live_mask, wavefunction, jnp.zeros_like(wavefunction))
    right_part = jnp.einsum("bij,bkj->bik", masked, right_env[0], preferred_element_type=jnp.float32).astype(jnp.bfloat16)
    factor = mpo_mask[0].astype(jnp.float32)
    product = jnp.einsum("bij,bjk->ibk", left_env[0], right_part, preferred_element_type=jnp.float32)
    row_share = lax.psum_scatter(
        (product * factor[None, :, None]).astype(jnp.bfloat16), "mpo", scatter_dimension=0, tiled=True
    ).astype(jnp.float32)
    global_rows = lax.axis_index("mpo") * row_count + jnp.arange(row_count, dtype=jnp.int32)
    live_rows = global_rows[:, None] < block_size[None, :]
    share_mask = live_rows[:, :, None] & live_cols[None, :, :]
    sigma_share = jnp.where(share_mask, row_share, jnp.zeros_like(row_share)).astype(jnp.bfloat16)
    return exchange_all(sigma_share, route_owner, route_block)


def route(peers, blocks, group_rows, width, owner_ref, block_ref, size_ref, sent_ref, info_ref, count):
    first_row = lax.axis_index("mpo") * (ROW_GROUPS * group_rows)
    spill_at = peers * SLOTS
    for i in range(spill_at + 2 * SPILL):
        info_ref[i] = -1
    for i in range(SPILL):
        sent_ref[blocks * PIECES + i] = -1
    for i in range(peers):
        count[i] = 0

    nowhere = TABLE - 2

    def one(step, spilled):
        b, k = blocks - 1 - step // PIECES, step % PIECES
        i = b * PIECES + k
        g, c = k // COL_PARTS, k % COL_PARTS
        size = size_ref[b]
        live = (first_row + g * group_rows < size) & (c * width < size)
        owner = owner_ref[0, b, k]
        pos = count[owner]
        code = block_ref[0, b, k] * PIECES + k
        direct = live & (pos < SLOTS)
        kept = live & (pos >= SLOTS) & (spilled < SPILL)
        sent_ref[i] = jnp.where(direct, owner * SLOTS + pos, -1)
        info_ref[jnp.where(direct, owner * SLOTS + pos, nowhere)] = code
        count[owner] = pos + direct.astype(jnp.int32)
        sent_ref[jnp.where(kept, blocks * PIECES + spilled, nowhere)] = i
        info_ref[jnp.where(kept, spill_at + spilled, nowhere)] = owner
        info_ref[jnp.where(kept, spill_at + SPILL + spilled, nowhere)] = code
        return spilled + (live & (pos >= SLOTS)).astype(jnp.int32)

    spilled = lax.fori_loop(0, blocks * PIECES, one, 0, unroll=PIECES)
    sent_ref[TABLE - 1] = (spilled > SPILL).astype(jnp.int32)


def term_kernel(first, plan, size_ref, mask_ref, wave_ref, left_ref, right_ref, *refs):
    tables = ()
    if plan:
        tables = (*refs[:2], size_ref, *refs[-10:-8], refs[-1])
        refs = refs[2:-10] + refs[-8:-1]
    wave, left, right, own, send, come, go = refs[-7:]
    results = refs[-7 - 2 * wave.shape[0] : -7]
    count, states, _ = wave.shape
    share = states // 2
    rows, width = share // ROW_GROUPS, states // COL_PARTS
    mine = lax.axis_index("mpo").astype(jnp.int32)
    arrive = []
    for n in range(count):
        arrive.append(
            [
                pltpu.make_async_copy(source.at[first + n], target.at[n], come.at[n, i])
                for i, (source, target) in enumerate(((wave_ref, wave), (right_ref, right), (left_ref, left)))
            ]
        )
        for copy in arrive[-1]:
            copy.start()
    leave = []
    if plan:
        route(*plan, *tables)
    row = lax.broadcasted_iota(jnp.int32, (states, states), 0)
    col = lax.broadcasted_iota(jnp.int32, (states, states), 1)
    for n in range(count):
        size = size_ref[first + n]
        active = mask_ref[0, first + n] != 0
        arrive[n][0].wait()
        masked = jnp.where((row < size) & (col < size), wave[n], jnp.zeros_like(wave[n]))
        arrive[n][1].wait()
        part = lax.dot_general(masked, right[n], (((1,), (1,)), ((), ())), preferred_element_type=jnp.float32)
        part = part.astype(jnp.bfloat16)
        arrive[n][2].wait()
        for which, (target, out_ref, half) in enumerate(((send, results[2 * n + 1], 1 - mine), (own, results[2 * n], mine))):
            start = pl.multiple_of(half * share, share)
            product = jnp.dot(left[n, pl.ds(start, share), :], part, preferred_element_type=jnp.float32)
            keep = (row[:share] + start < size) & (col[:share] < size) & active
            product = jnp.where(keep, product, 0.0).astype(jnp.bfloat16)
            for k in range(PIECES):
                g, c = k // COL_PARTS, k % COL_PARTS
                target[n, k * rows : (k + 1) * rows, :] = product[g * rows : (g + 1) * rows, c * width : (c + 1) * width]
            leave.append(pltpu.make_async_copy(target.at[n], out_ref, go.at[n, which]))
            leave[-1].start()
    for copy in leave:
        copy.wait()


def terms(first, count, sizes, mask, wave, left, right, plan, behind):
    blocks, states, _ = wave.shape
    group_rows, width = states // 2 // ROW_GROUPS, states // COL_PARTS
    rows = PIECES * group_rows
    out = jax.ShapeDtypeStruct((rows, width), jnp.bfloat16)
    table = jax.ShapeDtypeStruct((TABLE,), jnp.int32)
    peers = lax.axis_size("sector")
    scratch = [pltpu.VMEM((count, states, states), jnp.bfloat16)] * 3 + [pltpu.VMEM((count, rows, width), jnp.bfloat16)] * 2
    scratch += [pltpu.SemaphoreType.DMA((count, 3)), pltpu.SemaphoreType.DMA((count, 2))]
    if plan:
        scratch += [pltpu.SMEM((peers,), jnp.int32)]
    return pl.pallas_call(
        functools.partial(term_kernel, first, (peers, blocks, group_rows, width) if plan else None),
        in_specs=[SMEM] * 2 + [HBM] * 3 + [SMEM] * len(plan) + [ANY] * len(behind),
        out_specs=[HBM] * (2 * count) + [SMEM] * len(plan),
        out_shape=[out] * (2 * count) + [table] * len(plan),
        scratch_shapes=scratch,
        compiler_params=params(63),
        cost_estimate=pl.CostEstimate(flops=3000000000, bytes_accessed=1, transcendentals=0),
        name="terms",
    )(sizes, mask, wave, left, right, *plan, *behind)


def add(a, b):
    return (a.astype(jnp.float32) + b.astype(jnp.float32)).astype(jnp.bfloat16)


def fetch_spill(rows, blocks, sent_ref, sources, target, sems):
    for j in range(SPILL):
        index = sent_ref[blocks * PIECES + j]
        for b in range(SPILL_BLOCKS):

            def copy(b=b, j=j, index=index):
                at = pl.ds(pl.multiple_of((index - b * PIECES) * rows, rows), rows)
                return pltpu.make_async_copy(sources[b].at[at], target.at[pl.ds(j * rows, rows)], sems.at[j])

            yield (index >= b * PIECES) & (index < (b + 1) * PIECES), copy


def run_copies(copies):
    copies = list(copies)
    for step in ("start", "wait"):
        for there, copy in copies:

            @pl.when(there)
            def _(copy=copy, step=step):
                getattr(copy(), step)()


def spill_kernel(rows, blocks, sent_ref, info_ref, *refs):
    own_refs, other_refs = refs[:SPILL_BLOCKS], refs[SPILL_BLOCKS : 2 * SPILL_BLOCKS]
    out_ref, own, other, own_sems, other_sems = refs[2 * SPILL_BLOCKS + 1 :]
    run_copies(
        [*fetch_spill(rows, blocks, sent_ref, own_refs, own, own_sems), *fetch_spill(rows, blocks, sent_ref, other_refs, other, other_sems)]
    )
    out_ref[: SPILL * rows, :] = add(own[...], other[...])
    lane = lax.broadcasted_iota(jnp.int32, (INFO, TABLE), 1)
    table = jnp.where(lane == TABLE - 1, sent_ref[TABLE - 1], info_ref[...])
    out_ref[SPILL * rows :, :] = table.astype(jnp.float32).astype(jnp.bfloat16)


def join_kernel(rows, peers, count, *refs):
    near_ref, tables_ref, cross_ref, held, values, table, come, go = refs[-8:]
    me = lax.axis_index("sector").astype(jnp.int32)
    chunk = refs[0].shape[0]
    spill_at = peers * SLOTS
    arrive = [pltpu.make_async_copy(ref, held.at[pl.ds(i * chunk, chunk)], come.at[i]) for i, ref in enumerate(refs[:count])]
    for copy in arrive:
        copy.start()
    leave = []
    for i, copy in enumerate(arrive):
        copy.wait()
        at, info = pl.ds(i * chunk, chunk), pl.ds((i + 1) * chunk - INFO, INFO)
        leave.append(pltpu.make_async_copy(held.at[info], tables_ref.at[pl.ds(i * INFO, INFO)], go.at[count + i]))
        leave.append(pltpu.make_async_copy(held.at[at], near_ref.at[at], go.at[i]))
        leave[-2].start()
        leave[-1].start()
        values[i : i + 1, :] = held[(i + 1) * chunk - INFO : (i + 1) * chunk, :].astype(jnp.float32).astype(jnp.int32)[:1, :]
    copy = pltpu.make_async_copy(values, table, go.at[2 * count])
    copy.start()
    copy.wait()
    moves = []
    place = 0
    for i in range(count):
        for j in range(SPILL):
            owner = table[i, spill_at + j]
            there = (owner >= 0) & (owner // 4 == me // 4) & ((owner ^ me) & 2 == 2)
            fits = there & (place < CROSS)

            def move(i=i, j=j, place=place):
                to = pl.ds(pl.multiple_of(place * rows, rows), rows)
                sem = go.at[2 * count + 1 + i * SPILL + j]
                return pltpu.make_async_copy(held.at[pl.ds(i * chunk + j * rows, rows)], cross_ref.at[to], sem)

            moves.append((fits, move))
            place = place + there.astype(jnp.int32)
    run_copies(moves)
    for copy in leave:
        copy.wait()


def join(rows, peers, behind, *parts):
    chunk, width = parts[0].shape
    count = len(parts)
    return pl.pallas_call(
        functools.partial(join_kernel, rows, peers, count),
        in_specs=[ANY] * (count + len(behind)),
        out_specs=[HBM] * 3,
        out_shape=[jax.ShapeDtypeStruct((n, width), jnp.bfloat16) for n in (count * chunk, count * INFO, CROSS * rows)],
        scratch_shapes=[
            pltpu.VMEM((count * chunk, width), jnp.bfloat16),
            pltpu.VMEM((count, TABLE), jnp.int32),
            pltpu.SMEM((count, TABLE), jnp.int32),
            pltpu.SemaphoreType.DMA((count,)),
            pltpu.SemaphoreType.DMA((2 * count + 1 + count * SPILL,)),
        ],
        compiler_params=params(16),
        name="join",
    )(*parts, *behind)


def pack_kernel(first, rows, pairs, sent_ref, *refs):
    own_refs, other_refs = refs[:pairs], refs[pairs : 2 * pairs]
    out_ref, stage, sems = refs[-3:]
    done = 0
    copies = []
    for own_ref, other_ref in zip(own_refs, other_refs):
        count = own_ref.shape[0] // rows
        stage[done * rows : (done + count) * rows, :] = add(own_ref[...], other_ref[: count * rows, :])
        for k in range(done, done + count):
            slot = sent_ref[first * PIECES + k]

            def copy(k=k, slot=slot):
                to = pl.ds(pl.multiple_of(slot * rows, rows), rows)
                return pltpu.make_async_copy(stage.at[pl.ds(k * rows, rows)], out_ref.at[to], sems.at[k])

            copies.append((slot >= 0, copy))

            @pl.when(slot >= 0)
            def _(copy=copy):
                copy().start()

        done += count
    for there, copy in copies:

        @pl.when(there)
        def _(copy=copy):
            copy().wait()


def pack(first, sent, own, other, packed, rows, slots, behind):
    total, width = sum(x.shape[0] for x in own), own[0].shape[1]
    before = [] if packed is None else [packed]
    pairs = len(own)
    return pl.pallas_call(
        functools.partial(pack_kernel, first, rows, pairs),
        in_specs=[SMEM] + [VMEM] * (2 * pairs) + [HBM] * len(before) + [ANY] * len(behind),
        out_specs=HBM,
        out_shape=jax.ShapeDtypeStruct((slots * rows, width), jnp.bfloat16),
        scratch_shapes=[pltpu.VMEM((total, width), jnp.bfloat16), pltpu.SemaphoreType.DMA((total // rows,))],
        input_output_aliases={1 + 2 * pairs: 0} if before else {},
        compiler_params=params(16),
        name="pack",
    )(sent, *own, *other, *before, *behind)


def list_places(peers, blocks):
    begin = peers * (SLOTS + SPILL)
    return begin, begin + blocks * PIECES + 1, begin + 2 * blocks * PIECES + 1


def list_kernel(rows, peers, blocks, *refs):
    sets, (plan_ref, more_ref, lines, values, table, codes, count, cross, sems) = refs[:4], refs[4:]
    me = lax.axis_index("sector")
    quarter = peers // 4
    chunk = SPILL * rows + INFO
    slots, targets = peers * SLOTS, blocks * PIECES
    begin_at, middle_at, where_at = list_places(peers, blocks)
    copies = []
    for which, ref in enumerate(sets):
        for z in range(quarter):
            i = which * quarter + z
            copies.append(pltpu.make_async_copy(ref.at[pl.ds(z * INFO, INFO)], lines.at[i], sems.at[i]))
            copies[-1].start()
    for i in range(targets + 1):
        count[i] = 0
    for i, copy in enumerate(copies):
        copy.wait()
        values[i : i + 1, :] = lines[i].astype(jnp.float32).astype(jnp.int32)[:1, :]
    copy = pltpu.make_async_copy(values, table, sems.at[peers])
    copy.start()
    copy.wait()

    def note(i, code):
        to = jnp.where(code >= 0, code, targets)
        codes[i] = to
        count[to] += 1

    def source(j, more):
        apart = j ^ me
        line = ((apart & 1) * 2 + ((apart >> 1) & 1)) * quarter + (apart >> 2)
        for slot in range(SLOTS):
            note(j * SLOTS + slot, table[line, me * SLOTS + slot])
        for i in range(SPILL):
            owner = table[j, slots + i]
            note(slots + j * SPILL + i, jnp.where(owner == me, table[j, slots + SPILL + i], -1))
        return jnp.maximum(more, table[j, TABLE - 1])

    more = lax.fori_loop(0, peers, source, 0, unroll=4)

    for i in range(peers):
        cross[i] = 0

    def passed(line, place):
        which, z = line // quarter, line % quarter
        origin = me ^ (z * 4 + which % 2 * 2 + which // 2)
        place = jnp.where(z == 0, 0, place)
        for j in range(SPILL):
            owner = table[line, slots + j]
            change = (owner >= 0) & ((owner ^ origin) & 2 == 2)
            to = jnp.maximum(owner, 0) // 4 * 4 + origin % 4
            cross[to] += change.astype(jnp.int32)
            plan_ref[where_at + line * SPILL + j] = place
            place = place + (change & (owner // 4 == me // 4)).astype(jnp.int32)
        return place

    lax.fori_loop(0, peers, passed, 0, unroll=4)
    for i in range(peers):
        more = jnp.maximum(more, (cross[i] > CROSS).astype(jnp.int32))
    more_ref[0] = more

    def total(t, before):
        plan_ref[begin_at + t] = before
        after = before + count[t]
        count[t] = before
        return after

    lax.fori_loop(0, targets + 1, total, 0, unroll=True)

    def put(i, _):
        code = codes[i]
        place = count[code]
        plan_ref[place] = i
        count[code] = place + 1
        return 0

    lax.fori_loop(0, slots, put, 0, unroll=peers // 2)
    for t in range(targets):
        plan_ref[middle_at + t] = count[t]
    lax.fori_loop(slots, slots + peers * SPILL, put, 0, unroll=peers // 2)


def land_kernel(rows, peers, plan_ref, arrived_ref, *refs):
    sets, (out_ref, held, stage, sems, out_sems) = refs[:4], refs[4:]
    quarter = peers // 4
    chunk = SPILL * rows + INFO
    slots = peers * SLOTS
    blocks, share, states = stage.shape
    begin_at, middle_at, where_at = list_places(peers, blocks)
    width = states // COL_PARTS

    def at(start, unit=rows):
        return pl.ds(pl.multiple_of(start, unit), rows)

    def fetch(i, ref, start):
        place = i - slots
        return pltpu.make_async_copy(ref.at[at(start, 16)], held.at[at(place * rows)], sems.at[place])

    def begin(n, _):
        i = plan_ref[n]

        @pl.when(i >= slots)
        def _():
            source, j = (i - slots) // SPILL, (i - slots) % SPILL
            for which in range(4):

                @pl.when(source // quarter == which)
                def _(which=which):
                    place = jnp.minimum(plan_ref[where_at + i - slots], CROSS - 1)
                    start = place * rows if which % 2 else source % quarter * chunk + j * rows
                    fetch(i, sets[which], start).start()

        return 0

    lax.fori_loop(0, plan_ref[begin_at + blocks * PIECES], begin, 0)

    copies = []
    half = PIECES // 2
    for t in range(blocks):
        for k in range(PIECES):
            g, c = k // COL_PARTS, k % COL_PARTS
            first, last = plan_ref[begin_at + t * PIECES + k], plan_ref[begin_at + t * PIECES + k + 1]
            place = (t, slice(g * rows, (g + 1) * rows), slice(c * width, (c + 1) * width))

            middle = plan_ref[middle_at + t * PIECES + k]
            alone = (last == first + 1) & (middle == last)

            @pl.when(alone)
            def _(place=place, first=first):
                stage[place] = arrived_ref[at(plan_ref[first] * rows), :]

            @pl.when(jnp.logical_not(alone))
            def _(place=place, first=first, middle=middle, last=last):
                def direct(n, total):
                    return total + arrived_ref[at(plan_ref[n] * rows), :].astype(jnp.float32)

                def spilled(n, total):
                    i = plan_ref[n]
                    fetch(i, sets[0], 0).wait()
                    return total + held[at((i - slots) * rows), :].astype(jnp.float32)

                total = lax.fori_loop(first, middle, direct, jnp.zeros((rows, width), jnp.float32))
                stage[place] = lax.fori_loop(middle, last, spilled, total).astype(stage.dtype)

            if k % half == half - 1:
                strip = pl.ds(k // half * (share // 2), share // 2)
                copies.append(pltpu.make_async_copy(stage.at[t, strip], out_ref.at[t, strip], out_sems.at[len(copies)]))
                copies[-1].start()
    for copy in copies:
        copy.wait()


def two_halves(wavefunction, left_env, right_env, mpo_mask, block_size, route_owner, route_block):
    blocks, states, _ = wavefunction.shape
    share = states // 2
    rows = share // ROW_GROUPS
    width = states // COL_PARTS
    peers = lax.axis_size("sector")
    chunk = SPILL * rows + INFO

    def bf16(*shape):
        return jax.ShapeDtypeStruct(shape, jnp.bfloat16)

    def int32(*shape):
        return jax.ShapeDtypeStruct(shape, jnp.int32)

    def swap(x):
        return lax.ppermute(x, "mpo", [(0, 1), (1, 0)])

    def across(x, apart):
        return lax.ppermute(x, "sector", [(i, i ^ apart) for i in range(peers)])

    own, send, other = [], [], []

    def run(first, count, plan, behind):
        made = terms(first, count, block_size, mpo_mask, wavefunction, left_env[0], right_env[0], plan, behind)
        for n in range(count):
            own.append(made[2 * n])
            send.append(made[2 * n + 1])
            other.append(swap(send[-1]))
        return made[2 * count :]

    for b in range(SPILL_BLOCKS):
        tables = run(b, 1, [route_owner, route_block] if b == SPILL_BLOCKS - 1 else [], send[-1:])
    sent, info = tables
    run(SPILL_BLOCKS, blocks - SPILL_BLOCKS, [], send[-1:])

    spilled = pl.pallas_call(
        functools.partial(spill_kernel, rows, blocks),
        in_specs=[SMEM, VMEM] + [HBM] * (2 * SPILL_BLOCKS) + [ANY],
        out_specs=VMEM,
        out_shape=bf16(chunk, width),
        scratch_shapes=[pltpu.VMEM((SPILL * rows, width), jnp.bfloat16)] * 2
        + [pltpu.SemaphoreType.DMA((SPILL,))] * 2,
        compiler_params=params(63),
        name="spill",
    )(sent, info.reshape(1, TABLE), *own[:SPILL_BLOCKS], *other[:SPILL_BLOCKS], send[-1])
    last = blocks - 1
    along = [across(spilled, apart) for apart in range(4, peers, 4)]
    packed = pack(0, sent, own[:last], other[:last], None, rows, peers * SLOTS, [])
    packed = pack(last, sent, own[last:], other[last:], packed, rows, peers * SLOTS, [])
    near, tables, crossing = join(rows, peers, [packed], spilled, *along)
    tables_beside, tables_mate = across(tables, 2), across(tables, 1)
    tables = [tables, tables_beside, tables_mate, across(tables_beside, 1)]
    beside = across(crossing, 2)
    arrived = lax.all_to_all(packed.reshape(peers, SLOTS * rows, width), "sector", split_axis=0, concat_axis=0, tiled=True)
    arrived = arrived.reshape(peers * SLOTS * rows, width)

    pieces = peers * (SLOTS + SPILL)
    plan, more = pl.pallas_call(
        functools.partial(list_kernel, rows, peers, blocks),
        in_specs=[HBM] * 4,
        out_specs=[SMEM] * 2,
        out_shape=[int32(list_places(peers, blocks)[-1] + peers * SPILL), int32(1)],
        scratch_shapes=[
            pltpu.VMEM((peers, INFO, TABLE), jnp.bfloat16),
            pltpu.VMEM((peers, TABLE), jnp.int32),
            pltpu.SMEM((peers, TABLE), jnp.int32),
            pltpu.SMEM((pieces,), jnp.int32),
            pltpu.SMEM((blocks * PIECES + 1,), jnp.int32),
            pltpu.SMEM((peers,), jnp.int32),
            pltpu.SemaphoreType.DMA((peers + 1,)),
        ],
        compiler_params=params(16),
        cost_estimate=pl.CostEstimate(flops=17000000000, bytes_accessed=0, transcendentals=0),
        name="list",
    )(*tables)

    more = jnp.maximum(more, swap(more))
    beside, plan, more = lax.optimization_barrier((beside, plan, more))
    sets = [near, beside, across(near, 1), across(beside, 1)]

    def fast(plan, arrived, sets, *_):
        return pl.pallas_call(
            functools.partial(land_kernel, rows, peers),
            in_specs=[SMEM, VMEM] + [ANY] * 4,
            out_specs=HBM,
            out_shape=bf16(blocks, share, states),
            scratch_shapes=[
                pltpu.VMEM((peers * SPILL * rows, width), jnp.bfloat16),
                pltpu.VMEM((blocks, share, states), jnp.bfloat16),
                pltpu.SemaphoreType.DMA((peers * SPILL,)),
                pltpu.SemaphoreType.DMA((2 * blocks,)),
            ],
            compiler_params=params(16),
            name="land",
        )(plan, arrived, *sets)

    def slow(landed, own, other):
        sums = jnp.concatenate([add(a, b[: a.shape[0]]) for a, b in zip(own, other)], axis=0)
        sums = sums.reshape(blocks, ROW_GROUPS, COL_PARTS, rows, width).transpose(1, 3, 0, 2, 4)
        return exchange_all(sums.reshape(share, blocks, states), route_owner, route_block)

    landed = fast(plan, arrived, tuple(sets))
    return lax.cond(more[0] <= 0, lambda landed, own, other: landed, slow, landed, tuple(own), tuple(other))


def solution(mesh):
    placed = (
        P("sector", None, None),
        P("mpo", "sector", None, None),
        P("mpo", "sector", None, None),
        P("mpo", "sector"),
        P("sector"),
        P("mpo", "sector", None),
        P("mpo", "sector", None),
    )

    def per_device(wavefunction, *rest):
        states = wavefunction.shape[1]
        peers = mesh.shape["sector"]
        fits = (
            mesh.shape["mpo"] == 2
            and peers >= 8
            and peers & (peers - 1) == 0
            and wavefunction.shape[0] == SLOTS + SPILL_BLOCKS
            and states // COL_PARTS == TABLE
            and states // (2 * ROW_GROUPS) % 16 == 0
            and peers * SLOTS + 2 * SPILL < TABLE
        )
        return (two_halves if fits else general)(wavefunction, *rest)

    return jax.shard_map(per_device, mesh=mesh, in_specs=placed, out_specs=P("sector", "mpo", None), check_vma=False)
```
